32 devices in a mesh: dp: 8 (over y, x, core), mp: 4 (over z).
Axes of the slice: x: 2, y: 2, z: 4, core: 2. Of those that a mesh axis runs over, the one named last changes fastest.
Arguments:
- tokens: bfloat16 [1024, 8, 1024], P('mp', 'dp'), may hold values from -6 to 6
- memory: bfloat16 [1024, 8, 1024], P('mp', 'dp'), may hold values from -6 to 6
- self_qkv: bfloat16 [1024, 3, 1024], P(None, None, 'mp'), may hold values from -1 to 1
- self_out: bfloat16 [1024, 1024], P(None, 'mp'), may hold values from -0.75 to 0.75
- cross_q: bfloat16 [1024, 1024], P(None, 'mp'), may hold values from -1 to 1
- cross_kv: bfloat16 [1024, 2, 1024], P(None, None, 'mp'), may hold values from -1 to 1
- cross_out: bfloat16 [1024, 1024], P(None, 'mp'), may hold values from -1 to 1
- ffn_in: bfloat16 [1024, 4096], P(None, 'mp'), may hold values from -0.1875 to 0.1875
- ffn_out: bfloat16 [1024, 4096], P(None, 'mp'), may hold values from -0.375 to 0.375
- ln_gain: float32 [3, 1024], replicated, may hold values from 0.5 to 1.5
- ln_bias: float32 [3, 1024], replicated, may hold values from -1.5 to 1.5
- cotangent: bfloat16 [1024, 8, 1024], P('mp', 'dp'), may hold values from -6 to 6
Outputs:
- mixed: bfloat16 [1024, 8, 1024], P('mp', 'dp')
- token_grad: bfloat16 [1024, 8, 1024], P('mp', 'dp')
- memory_grad: bfloat16 [1024, 8, 1024], P('mp', 'dp')
- self_qkv_grad: float32 [1024, 3, 1024], P('dp', None, 'mp')
- self_out_grad: float32 [1024, 1024], P('dp', 'mp')
- cross_q_grad: float32 [1024, 1024], P('dp', 'mp')
- cross_kv_grad: float32 [1024, 2, 1024], P('dp', None, 'mp')
- cross_out_grad: float32 [1024, 1024], P('dp', 'mp')
- ffn_in_grad: float32 [1024, 4096], P('dp', 'mp')
- ffn_out_grad: float32 [1024, 4096], P('dp', 'mp')
- gain_grad: float32 [3, 1024], replicated
- bias_grad: float32 [3, 1024], replicated
The draws below stay inside these ranges and needn't reach their ends.
All inputs are finite; a program needn't handle non-finite values.
Results may differ from the reference program's by a relative error of at most 0.025.
Values may be sent and summed in bfloat16 or wider, within the bound.
No kernel may reach another device: no remote copies, remote signals or barrier semaphores. Data moves between devices by JAX's collectives and lax.ppermute only.
A program may use at most 192 MiB of HBM per device.

```python
import math
import jax
import jax.numpy as jnp
from jax import lax

D = 1024
HEADS = 16
HD = 64
FF = 4096
LEN = 1024
MEM = 1024
PAIRS = 8


def spread_draw(key, shape, scale):
    values = jnp.clip(jax.random.normal(key, shape, jnp.float32) * scale, -6.0 * scale, 6.0 * scale)
    return values


def draw_tokens(key, part):
    key = jax.random.fold_in(key, 11)
    return spread_draw(key, (LEN, PAIRS, D), 1.0).astype(jnp.bfloat16)


def draw_memory(key, part):
    key = jax.random.fold_in(key, 12)
    return spread_draw(key, (MEM, PAIRS, D), 1.0).astype(jnp.bfloat16)


def draw_self_qkv(key, part):
    key = jax.random.fold_in(key, 13)
    return spread_draw(key, (D, 3, D), (D // 2) ** (-0.5)).astype(jnp.bfloat16)


def draw_cross_q(key, part):
    key = jax.random.fold_in(key, 14)
    return spread_draw(key, (D, D), (D // 4) ** (-0.5)).astype(jnp.bfloat16)


def draw_cross_kv(key, part):
    key = jax.random.fold_in(key, 15)
    return spread_draw(key, (D, 2, D), D ** (-0.5)).astype(jnp.bfloat16)


def spiked(values, rng, source, target, blocks, factor):
    def block_of(position):
        return (jnp.arange(values.shape[position]) // (values.shape[position] // blocks)).reshape((-1,) + (1,) * (values.ndim - 1 - position))

    near = jax.random.permutation(rng, blocks)[block_of(target)]
    other_side = (block_of(target) + blocks // 2) % blocks
    return jnp.where((block_of(source) == near) | (block_of(source) == other_side), factor * values, values)


def level_of(key, shape, shards, smallest, top_value):
    factor_of, own = 1.0, jax.random.fold_in(key, 6)
    for dim, blocks in shards:
        heights = jnp.exp(jax.random.uniform(jax.random.fold_in(own, dim), (blocks,), jnp.float32, smallest / len(shards), top_value / len(shards)))
        factor_of = factor_of * jnp.repeat(heights, shape[dim] // blocks).reshape([-1 if axis == dim else 1 for axis in range(len(shape))])
    return factor_of


def scatter_about(own_key, dims, scale, most, cuts=(), held_as=jnp.bfloat16):
    loudness = level_of(own_key, dims, cuts, -0.22, 0.18) if cuts else 1.0
    array = jax.random.normal(own_key, dims, jnp.float32) * scale * loudness
    return jnp.minimum(jnp.maximum(array, -most), most).astype(held_as)


def heavy_noise(stream_key, dims, deviation, most, pieces, heavy, kind=jnp.bfloat16):
    array = deviation * jax.random.normal(stream_key, dims, jnp.float32)
    if pieces:
        array = array * level_of(stream_key, dims, pieces, -0.22, 0.18)
    return jnp.clip(spiked(array, jax.random.fold_in(stream_key, 3), *heavy), -most, most).astype(kind)


def setup_inputs(seed: int = 0) -> dict:
    seeds = jax.random.split(jax.random.key(seed), 13)
    return {
        "tokens": draw_tokens(jax.random.fold_in(seeds[12], 71), 0),
        "memory": draw_memory(jax.random.fold_in(seeds[12], 71), 0),
        "self_qkv": draw_self_qkv(jax.random.fold_in(seeds[12], 71), 0),
        "self_out": scatter_about(seeds[3], (D, D), (D // 16) ** -0.5, 0.75, ((1, 4),)),
        "cross_q": draw_cross_q(jax.random.fold_in(seeds[12], 71), 0),
        "cross_kv": draw_cross_kv(jax.random.fold_in(seeds[12], 71), 0),
        "cross_out": scatter_about(seeds[6], (D, D), (D // 32) ** -0.5, 1.0, ((1, 4),)),
        "ffn_in": scatter_about(seeds[7], (D, FF), D ** -0.5, 0.1875, ((1, 4),)),
        "ffn_out": scatter_about(seeds[8], (D, FF), (FF // 16) ** -0.5, 0.375, ((1, 4),)),
        "ln_gain": jnp.clip(1.0 + 0.1 * jax.random.normal(seeds[9], (3, D), jnp.float32), 0.5, 1.5),
        "ln_bias": scatter_about(seeds[10], (3, D), 0.3, 1.5, (), jnp.float32),
        "cotangent": heavy_noise(seeds[11], (LEN, PAIRS, D), 1.0, 6.0, ((0, 4), (1, 8)), (1, 2, 8, 2.0)),
    }


@jax.custom_vjp
def low(v):
    return lax.optimization_barrier(v.astype(jnp.bfloat16)).astype(jnp.float32)

@jax.custom_vjp
def low_back(v):
    return v

def low_keep(v):
    return (low(v), None)

def low_pass(kept, grad):
    return (grad,)

def back_keep(v):
    return (v, None)

def back_low(kept, grad):
    return (low(grad),)
low.defvjp(low_keep, low_pass)
low_back.defvjp(back_keep, back_low)
alpha_scale = 300.0 ** 0.25
norm_eps = 1e-05

def layer_norm(value, gain, bias):
    center = value - lax.optimization_barrier(jnp.mean(value, axis=-1, keepdims=True))
    spread = lax.optimization_barrier(jnp.mean(center * center, axis=-1, keepdims=True))
    return center * lax.rsqrt(spread + norm_eps) * gain + bias

def dense(left, weight):
    return jnp.dot(left, weight, precision=lax.Precision.HIGHEST)

def attend(queries, keys, values, causal):
    seq = queries.shape[0]
    block = min(512, seq)
    factor = 1.0 / math.sqrt(HD)

    def one_block(begin):
        query_block = lax.dynamic_slice_in_dim(queries, begin, block, 0)
        scores = jnp.einsum('qhe,khe->hqk', query_block, keys, precision=lax.Precision.HIGHEST) * factor
        scores = low_back(scores)
        if causal:
            rows_at = begin + jnp.arange(block, dtype=jnp.int32)[:, None]
            cols_at = jnp.arange(keys.shape[0], dtype=jnp.int32)[None, :]
            scores = jnp.where(cols_at <= rows_at, scores, -1000000000.0)
        norm_log = jax.nn.logsumexp(scores, axis=-1, keepdims=True)
        probs = low(jnp.exp(scores - norm_log))
        return jnp.einsum('hqk,khe->qhe', probs, values, precision=lax.Precision.HIGHEST)
    begins = (jnp.arange(seq // block, dtype=jnp.int32) * block).astype(jnp.int32)
    result = lax.map(jax.checkpoint(one_block), begins)
    return result.reshape(seq, HEADS * HD)

def forward(x, mem, self_qkv, self_out, cross_q, cross_kv, cross_out, ffn_in, ffn_out, ln_gain, ln_bias):
    seq = x.shape[0]
    span = mem.shape[0]
    projected = low_back(low(dense(x, self_qkv.reshape(D, 3 * D))))
    queries = projected[:, :D].reshape(seq, HEADS, HD)
    keys = projected[:, D:2 * D].reshape(seq, HEADS, HD)
    values = projected[:, 2 * D:].reshape(seq, HEADS, HD)
    attended = low_back(low(attend(queries, keys, values, True)))
    self_branch = low_back(dense(attended, self_out.T))
    first = layer_norm(alpha_scale * x + self_branch, ln_gain[0], ln_bias[0])
    cross_queries = low_back(low(dense(low(first), cross_q))).reshape(seq, HEADS, HD)
    cross_pair = low_back(low(dense(mem, cross_kv.reshape(D, 2 * D))))
    cross_keys = cross_pair[:, :D].reshape(span, HEADS, HD)
    cross_values = cross_pair[:, D:].reshape(span, HEADS, HD)
    cross_attended = low_back(low(attend(cross_queries, cross_keys, cross_values, False)))
    cross_branch = low_back(dense(cross_attended, cross_out.T))
    second = layer_norm(alpha_scale * first + cross_branch, ln_gain[1], ln_bias[1])
    hidden = low_back(dense(low(second), ffn_in))
    activation = low_back(low(jax.nn.gelu(hidden, approximate=True)))
    ffn_branch = low_back(dense(activation, ffn_out.T))
    return layer_norm(alpha_scale * second + ffn_branch, ln_gain[2], ln_bias[2])

def reference(tokens, memory, self_qkv, self_out, cross_q, cross_kv, cross_out, ffn_in, ffn_out, ln_gain, ln_bias, cotangent):
    weights = tuple((w.astype(jnp.float32) for w in (self_qkv, self_out, cross_q, cross_kv, cross_out, ffn_in, ffn_out, ln_gain, ln_bias)))
    token_rows = jnp.transpose(tokens.astype(jnp.float32), (1, 0, 2))
    memory_rows = jnp.transpose(memory.astype(jnp.float32), (1, 0, 2))
    grad_rows = jnp.transpose(cotangent.astype(jnp.float32), (1, 0, 2))

    def step(carry, item):
        x, mem, incoming = item
        output, pull = jax.vjp(forward, x, mem, *weights)
        grads = pull(incoming)
        carry = tuple((c + g for c, g in zip(carry, grads[2:])))
        return (carry, (output, grads[0], grads[1]))
    start_grads = tuple((jnp.zeros_like(w) for w in weights))
    totals, (outputs, token_grads, memory_grads) = lax.scan(step, start_grads, (token_rows, memory_rows, grad_rows))
    mixed = jnp.transpose(outputs, (1, 0, 2)).astype(jnp.bfloat16)
    token_grad = jnp.transpose(token_grads, (1, 0, 2)).astype(jnp.bfloat16)
    memory_grad = jnp.transpose(memory_grads, (1, 0, 2)).astype(jnp.bfloat16)
    return (mixed, token_grad, memory_grad, totals[0], totals[1], totals[2], totals[3], totals[4], totals[5], totals[6], totals[7], totals[8])
```

```python
import functools
import math

import jax
import jax.numpy as jnp
from jax import lax
from jax.experimental import pallas as pl
from jax.experimental.pallas import tpu as pltpu
from jax.sharding import PartitionSpec as P

HD = 64
CELLS = 8
BITS = (2, 4)
LOW = jnp.bfloat16
WIDE = jnp.float32
SELF_BLOCKS = (512, 512)
CROSS_BLOCKS = (1024, 256)
SELF_BACK_BLOCKS = (512, 512)
CROSS_BACK_BLOCKS = (1024, 256)
VMEM_LIMIT = 56 * 2**20

alpha_scale = 300.0**0.25
norm_eps = 1e-05

NN = (((1,), (0,)), ((), ()))
NT = (((1,), (1,)), ((), ()))
TN = (((0,), (0,)), ((), ()))


def dense(left, weight):
    return jnp.einsum("td,df->tf", left, weight, preferred_element_type=WIDE)


def weight_grad(left, grad):
    return jnp.einsum("td,tf->df", left, grad, preferred_element_type=WIDE).astype(LOW)


def back_dense(grad, weight):
    return jnp.einsum("tf,df->td", grad, weight, preferred_element_type=WIDE)


def mm(left, right, dims):
    return lax.dot_general(left, right, dims, preferred_element_type=WIDE)


def keep_head(value, head):
    at = lax.broadcasted_iota(jnp.int32, value.shape, 1) // HD
    return jnp.where(at == head, value, jnp.zeros_like(value))


def masked(scores, key_begin, query_begin):
    key_at = lax.broadcasted_iota(jnp.int32, scores.shape, 0) + key_begin
    query_at = lax.broadcasted_iota(jnp.int32, scores.shape, 1) + query_begin
    return jnp.where(key_at <= query_at, scores, -1000000000.0)


def key_blocks(body, carry, query_block, key_block, keys, causal):
    if not causal:
        for j in range(keys // key_block):
            carry = body(j, carry, False)
        return carry
    per = query_block // key_block
    begin = pl.program_id(1) * per
    carry = lax.fori_loop(0, begin, lambda j, c: body(j, c, False), carry)
    for e in range(per):
        carry = body(begin + e, carry, True)
    return carry


def attend_kernel(q_ref, k_ref, v_ref, o_ref, lse_ref, *, key_block, causal):
    query_block = q_ref.shape[0]
    query_begin = pl.program_id(1) * query_block
    q = q_ref[...] * jnp.asarray(1.0 / math.sqrt(HD), LOW)

    def body(j, carry, diagonal):
        tops, sums, acc = carry[:2], carry[2:4], carry[4]
        at = pl.multiple_of(j * key_block, key_block)
        k, v = k_ref[pl.ds(at, key_block), :], v_ref[pl.ds(at, key_block), :]
        new_tops, new_sums, shrink, parts = [], [], [], []
        for head in (0, 1):
            s = mm(keep_head(k, head), q, NT)
            if diagonal:
                s = masked(s, j * key_block, query_begin)
            top = jnp.maximum(tops[head], jnp.max(s, axis=0, keepdims=True))
            p = jnp.exp(s - top)
            factor = jnp.exp(tops[head] - top)
            new_tops.append(top)
            new_sums.append(sums[head] * factor + jnp.sum(p, axis=0, keepdims=True))
            shrink.append(factor)
            parts.append(mm(keep_head(v, head), p.astype(LOW), TN))
        upper = lax.broadcasted_iota(jnp.int32, acc.shape, 0) < HD
        acc = acc * jnp.where(upper, shrink[0], shrink[1]) + (parts[0] + parts[1])
        return (*new_tops, *new_sums, acc)

    low = jnp.full((1, query_block), -1e30, WIDE)
    zero = jnp.zeros((1, query_block), WIDE)
    start = (low, low, zero, zero, jnp.zeros((2 * HD, query_block), WIDE))
    top0, top1, sum0, sum1, acc = key_blocks(
        body, start, query_block, key_block, k_ref.shape[0], causal
    )
    upper = lax.broadcasted_iota(jnp.int32, acc.shape, 0) < HD
    o_ref[...] = (acc * jnp.where(upper, 1.0 / sum0, 1.0 / sum1)).T.astype(LOW)
    lse_ref[0] = jnp.concatenate(
        [top0 + jnp.log(sum0), top1 + jnp.log(sum1), jnp.zeros((6, query_block), WIDE)], axis=0
    )


def attend_back_kernel(
    q_ref, g_ref, o_ref, lse_ref, k_ref, v_ref, dq_ref, dk_ref, dv_ref, dk_acc, dv_acc, *, key_block, causal
):
    query_block = q_ref.shape[0]
    query_begin = pl.program_id(1) * query_block

    @pl.when(pl.program_id(1) == 0)
    def _():
        dk_acc[...] = jnp.zeros_like(dk_acc)
        dv_acc[...] = jnp.zeros_like(dv_acc)

    q = q_ref[...] * jnp.asarray(1.0 / math.sqrt(HD), LOW)
    g = g_ref[...]
    q_heads = [keep_head(q, head) for head in (0, 1)]
    g_heads = [keep_head(g, head) for head in (0, 1)]
    picks = lax.broadcasted_iota(jnp.int32, (8, 2 * HD), 1) // HD
    picks = (picks == lax.broadcasted_iota(jnp.int32, (8, 2 * HD), 0)).astype(WIDE)
    inner = lax.dot_general(
        picks,
        g.astype(WIDE) * o_ref[...].astype(WIDE),
        NT,
        precision=lax.Precision.HIGHEST,
        preferred_element_type=WIDE,
    )
    lse = lse_ref[0]

    def body(j, dq, diagonal):
        at = pl.multiple_of(j * key_block, key_block)
        k, v = k_ref[pl.ds(at, key_block), :], v_ref[pl.ds(at, key_block), :]
        dk, dv = dk_acc[pl.ds(at, key_block), :], dv_acc[pl.ds(at, key_block), :]
        for head in (0, 1):
            k_head = keep_head(k, head)
            s = mm(k_head, q, NT)
            if diagonal:
                s = masked(s, j * key_block, query_begin)
            p = jnp.exp(s - lse[head : head + 1])
            dp = mm(keep_head(v, head), g, NT)
            ds = (p * (dp - inner[head : head + 1])).astype(LOW)
            dv = dv + mm(p.astype(LOW), g_heads[head], NN)
            dk = dk + mm(ds, q_heads[head], NN)
            dq = dq + mm(k_head, ds, TN)
        dk_acc[pl.ds(at, key_block), :] = dk
        dv_acc[pl.ds(at, key_block), :] = dv
        return dq

    dq = key_blocks(
        body, jnp.zeros((2 * HD, query_block), WIDE), query_block, key_block, k_ref.shape[0], causal
    )
    dq_ref[...] = (dq * (1.0 / math.sqrt(HD))).T.astype(LOW)

    @pl.when(pl.program_id(1) == pl.num_programs(1) - 1)
    def _():
        dk_ref[...] = dk_acc[...].astype(LOW)
        dv_ref[...] = dv_acc[...].astype(LOW)


def columns_of(rows, first, whole):
    if whole:
        return pl.BlockSpec((rows, 2 * HD), lambda p, i: (0, first + p))
    return pl.BlockSpec((rows, 2 * HD), lambda p, i: (i, first + p))


def attend(width, queries, keys, values, causal, query_block, key_block):
    seq, span = queries[0].shape[0], keys[0].shape[0]
    pairs = width // (2 * HD)
    return pl.pallas_call(
        functools.partial(attend_kernel, key_block=key_block, causal=causal),
        grid=(pairs, seq // query_block),
        in_specs=[
            columns_of(query_block, queries[1], False),
            columns_of(span, keys[1], True),
            columns_of(span, values[1], True),
        ],
        out_specs=[
            columns_of(query_block, 0, False),
            pl.BlockSpec((1, 8, query_block), lambda p, i: (p, 0, i)),
        ],
        out_shape=[
            jax.ShapeDtypeStruct((seq, width), LOW),
            jax.ShapeDtypeStruct((pairs, 8, seq), WIDE),
        ],
        compiler_params=pltpu.CompilerParams(vmem_limit_bytes=VMEM_LIMIT),
        cost_estimate=pl.CostEstimate(
            flops=8 * seq * span * width, bytes_accessed=8 * seq * width, transcendentals=0
        ),
        name="attend",
    )(queries[0], keys[0], values[0])


def attend_back(width, queries, keys, values, grad, result, lse, causal, query_block, key_block):
    seq, span = queries[0].shape[0], keys[0].shape[0]
    pairs = width // (2 * HD)
    whole = columns_of(span, 0, True)
    return pl.pallas_call(
        functools.partial(attend_back_kernel, key_block=key_block, causal=causal),
        grid=(pairs, seq // query_block),
        in_specs=[
            columns_of(query_block, queries[1], False),
            columns_of(query_block, 0, False),
            columns_of(query_block, 0, False),
            pl.BlockSpec((1, 8, query_block), lambda p, i: (p, 0, i)),
            columns_of(span, keys[1], True),
            columns_of(span, values[1], True),
        ],
        out_specs=[columns_of(query_block, 0, False), whole, whole],
        out_shape=[
            jax.ShapeDtypeStruct((seq, width), LOW),
            jax.ShapeDtypeStruct((span, width), LOW),
            jax.ShapeDtypeStruct((span, width), LOW),
        ],
        scratch_shapes=[pltpu.VMEM((span, 2 * HD), WIDE), pltpu.VMEM((span, 2 * HD), WIDE)],
        compiler_params=pltpu.CompilerParams(vmem_limit_bytes=VMEM_LIMIT),
        cost_estimate=pl.CostEstimate(
            flops=16 * seq * span * width, bytes_accessed=16 * seq * width, transcendentals=0
        ),
        name="attend_back",
    )(queries[0], grad, result, lse, keys[0], values[0])


def normalized(value):
    center = value - jnp.mean(value, axis=-1, keepdims=True)
    scale = lax.rsqrt(jnp.mean(center * center, axis=-1, keepdims=True) + norm_eps)
    return center * scale, scale


def norm_back(grad, gain, n, scale):
    e = grad * gain
    mean_e = jnp.mean(e, axis=-1, keepdims=True)
    mean_en = jnp.mean(e * n, axis=-1, keepdims=True)
    terms = jnp.concatenate(
        [jnp.sum(grad * n, axis=0, keepdims=True), jnp.sum(grad, axis=0, keepdims=True)], axis=0
    )
    return (e - mean_e - n * mean_en) * scale, terms


def gelu_with_slope(value):
    c = math.sqrt(2.0 / math.pi)
    square = value * value
    t = jnp.tanh(c * value * (1.0 + 0.044715 * square))
    half = 0.5 * (1.0 + t)
    slope = half + 0.5 * value * (1.0 - t * t) * (c * (1.0 + 3 * 0.044715 * square))
    return value * half, slope


def cell_copies(parts, first, target, sems, pick):
    cell = lax.rem(lax.axis_index("dp"), CELLS)
    rows = target.shape[-2] // CELLS
    copies = []
    for j in range(CELLS):
        part = parts[(j & 1) * 2 + (1 if j & (6 - first) else 0)].at[1 if j & first else 0]
        at = pl.multiple_of(jnp.bitwise_xor(cell, j) * rows, rows)
        copies.append(pltpu.make_async_copy(*pick(part, target, pl.ds(at, rows)), sems.at[j]))
    return copies


def start_all(copies):
    for copy in copies:
        copy.start()


def wait_all(copies):
    for copy in copies:
        copy.wait()


def enter_cross_kernel(
    tokens_ref, gain_ref, bias_ref, *refs, width, count
):
    attended, refs = refs[:count], refs[count:]
    parts, refs = refs[:4], refs[4:]
    n_ref, scale_ref, low_ref = refs[:3]
    queries, (weights, sems) = refs[3 : 3 + count], refs[3 + count :]
    copies = cell_copies(parts, 2, weights, sems, lambda part, to, at: (part, to.at[:, at, :]))
    shards = [jnp.bitwise_xor(lax.axis_index("mp"), k) for k in range(count)]
    start_all(copies)
    value = alpha_scale * tokens_ref[...].astype(WIDE)
    wait_all(copies)
    for k in range(count):
        value = value + mm(attended[k][...], weights[shards[k], :, :width], NT)
    n, scale = normalized(value)
    n_ref[...] = n
    scale_ref[...] = jnp.broadcast_to(scale, scale_ref.shape)
    low = (n * gain_ref[0:1, :] + bias_ref[0:1, :]).astype(LOW)
    low_ref[...] = low
    for k in range(count):
        queries[k][...] = mm(low, weights[shards[k], :, width:], NN).astype(LOW)


def leave_cross_kernel(
    cross_grad_ref, gain_ref, n_ref, scale_ref, *refs, width, count
):
    queries, refs = refs[:count], refs[count:]
    parts, refs = refs[:4], refs[4:]
    self_grad_ref, low_ref, terms_ref = refs[:3]
    grads, (weights, sems) = refs[3 : 3 + count], refs[3 + count :]
    copies = cell_copies(parts, 2, weights, sems, lambda part, to, at: (part, to.at[:, at, :]))
    shards = [jnp.bitwise_xor(lax.axis_index("mp"), k) for k in range(count)]
    start_all(copies)
    grad = alpha_scale * cross_grad_ref[...]
    wait_all(copies)
    for k in range(count):
        grad = grad + mm(queries[k][...], weights[shards[k], :, width:], NT)
    self_grad, terms_ref[...] = norm_back(grad, gain_ref[0:1, :], n_ref[...], scale_ref[:, :1])
    self_grad_ref[...] = self_grad
    low = self_grad.astype(LOW)
    low_ref[...] = low
    for k in range(count):
        grads[k][...] = mm(low, weights[shards[k], :, :width], NN).astype(LOW)


def feed_forward_kernel(
    first_n_ref, cotangent_ref, gain_ref, bias_ref, *refs, width, count
):
    attended, refs = refs[:count], refs[count:]
    parts, refs = (refs[:4], refs[4:8]), refs[8:]
    mixed_ref, second_low_ref, third_low_ref, cross_grad_ref, cross_low_ref, terms_ref = refs[:6]
    act_ref, hidden_grad_ref = refs[6:8]
    grads, refs = refs[8 : 8 + count], refs[8 + count :]
    w_in, w_out, w_cross, slope_ref, sum_ref, in_sems, out_sems, cross_sems = refs
    hidden = w_in.shape[2]
    chunk = min(512, hidden)
    half = count // 2

    shards = [jnp.bitwise_xor(lax.axis_index("mp"), k) for k in range(count)]

    cross_copies = []
    for h in range(2):
        cross_copies += cell_copies(
            parts[h],
            BITS[h],
            w_cross,
            cross_sems.at[h],
            lambda part, to, at: (part.at[:, :, 2 * hidden :], to.at[pl.ds(h * half, half), at, :]),
        )
    start_all(cross_copies)
    in_copies, out_copies = [], []
    for s in range(count):
        h = s // half
        in_copies.append(
            cell_copies(
                parts[h],
                BITS[h],
                w_in,
                in_sems.at[s],
                lambda part, to, at: (part.at[s % half, :, :hidden], to.at[s, at, :]),
            )
        )
        out_copies.append(
            cell_copies(
                parts[h],
                BITS[h],
                w_out,
                out_sems.at[s],
                lambda part, to, at: (part.at[s % half, :, hidden : 2 * hidden], to.at[s, at, :]),
            )
        )
        start_all(in_copies[s])
        start_all(out_copies[s])

    second = alpha_scale * (first_n_ref[...] * gain_ref[0:1, :] + bias_ref[0:1, :])
    wait_all(cross_copies)
    for k in range(count):
        second = second + mm(attended[k][...], w_cross[shards[k]], NT)
    second_n, second_scale = normalized(second)
    second = second_n * gain_ref[1:2, :] + bias_ref[1:2, :]
    second_low = second.astype(LOW)
    second_low_ref[...] = second_low
    sum_ref[...] = alpha_scale * second
    for k in range(count):
        wait_all(in_copies[k])
        for begin in range(0, hidden, chunk):
            cut = slice(begin, begin + chunk)
            value = mm(second_low, w_in[k, :, cut], NN)
            act, slope = gelu_with_slope(value)
            slope_ref[k, :, cut] = slope
            act_ref[k, :, cut] = act.astype(LOW)
        wait_all(out_copies[k])
        sum_ref[...] += mm(act_ref[k], w_out[k], NT)
    third_n, third_scale = normalized(sum_ref[...])
    mixed_ref[...] = (third_n * gain_ref[2:3, :] + bias_ref[2:3, :]).astype(LOW)
    third_grad, third_terms = norm_back(
        cotangent_ref[...].astype(WIDE), gain_ref[2:3, :], third_n, third_scale
    )
    third_low = third_grad.astype(LOW)
    third_low_ref[...] = third_low
    sum_ref[...] = alpha_scale * third_grad
    for k in range(count):
        for begin in range(0, hidden, chunk):
            cut = slice(begin, begin + chunk)
            act_grad = mm(third_low, w_out[k, :, cut], NN).astype(LOW).astype(WIDE)
            hidden_grad_ref[k, :, cut] = (act_grad * slope_ref[k, :, cut]).astype(LOW)
        sum_ref[...] += mm(hidden_grad_ref[k], w_in[k], NT)
    cross_grad, second_terms = norm_back(sum_ref[...], gain_ref[1:2, :], second_n, second_scale)
    terms_ref[...] = jnp.concatenate([second_terms, third_terms], axis=0)
    cross_grad_ref[...] = cross_grad
    cross_low = cross_grad.astype(LOW)
    cross_low_ref[...] = cross_low
    for k in range(count):
        grads[k][...] = mm(cross_low, w_cross[shards[k]], NN).astype(LOW)


def call(kernel, operands, streamed, results, scratch, flops, name):
    here, there = pl.BlockSpec(memory_space=pltpu.VMEM), pl.BlockSpec(memory_space=pl.ANY)
    arrays = [*operands, *streamed]
    size = sum(v.size * v.dtype.itemsize for v in arrays)
    return pl.pallas_call(
        kernel,
        in_specs=[here] * len(operands) + [there] * len(streamed),
        out_specs=[here] * len(results),
        out_shape=[jax.ShapeDtypeStruct(shape, dtype) for shape, dtype in results],
        scratch_shapes=scratch,
        compiler_params=pltpu.CompilerParams(vmem_limit_bytes=VMEM_LIMIT),
        cost_estimate=pl.CostEstimate(flops=flops, bytes_accessed=size, transcendentals=0),
        name=name,
    )(*arrays)


def enter_cross(tokens, gain, bias, attended, parts):
    rows, model = tokens.shape
    count, width = len(attended), attended[0].shape[1]
    return call(
        functools.partial(enter_cross_kernel, width=width, count=count),
        [tokens, gain, bias, *attended],
        parts,
        [((rows, model), WIDE), ((rows, 128), WIDE), ((rows, model), LOW)]
        + [((rows, width), LOW)] * count,
        [
            pltpu.VMEM((count, model, 2 * width), LOW),
            pltpu.SemaphoreType.DMA((CELLS,)),
        ],
        4 * rows * model * width * count,
        "enter_cross",
    )


def leave_cross(cross_grad, gain, n, scale, queries, parts):
    rows, model = n.shape
    count, width = len(queries), queries[0].shape[1]
    return call(
        functools.partial(leave_cross_kernel, width=width, count=count),
        [cross_grad, gain, n, scale, *queries],
        parts,
        [((rows, model), WIDE), ((rows, model), LOW), ((2, model), WIDE)]
        + [((rows, width), LOW)] * count,
        [
            pltpu.VMEM((count, model, 2 * width), LOW),
            pltpu.SemaphoreType.DMA((CELLS,)),
        ],
        4 * rows * model * width * count,
        "leave_cross",
    )


def feed_forward(first_n, cotangent, gain, bias, attended, hidden, parts):
    rows, model = first_n.shape
    count, width = len(attended), attended[0].shape[1]
    sems = pltpu.SemaphoreType.DMA((count, CELLS))
    return call(
        functools.partial(feed_forward_kernel, width=width, count=count),
        [first_n, cotangent, gain, bias, *attended],
        [*parts[0], *parts[1]],
        [
            ((rows, model), LOW),
            ((rows, model), LOW),
            ((rows, model), LOW),
            ((rows, model), WIDE),
            ((rows, model), LOW),
            ((4, model), WIDE),
            ((count, rows, hidden), LOW),
            ((count, rows, hidden), LOW),
        ]
        + [((rows, width), LOW)] * count,
        [
            pltpu.VMEM((count, model, hidden), LOW),
            pltpu.VMEM((count, model, hidden), LOW),
            pltpu.VMEM((count, model, width), LOW),
            pltpu.VMEM((count, rows, hidden), WIDE),
            pltpu.VMEM((rows, model), WIDE),
            sems,
            sems,
            pltpu.SemaphoreType.DMA((2, CELLS)),
        ],
        8 * rows * model * hidden * count,
        "feed_forward",
    )


def weight_grads_kernel(*refs, other_core):
    count = (len(refs) - 2) // 2
    lefts, rights, out_ref, turned = refs[:count], refs[count:-2], refs[-2], refs[-1]
    block = turned.shape[1] // (CELLS // 2)

    @pl.when(pl.program_id(0) == 0)
    def _():
        cell = lax.rem(lax.axis_index("dp"), CELLS)
        for i, left in enumerate(lefts):
            for c in range(CELLS // 2):
                at = jnp.bitwise_xor(cell, 2 * c + other_core) * block
                columns = left[:, pl.ds(pl.multiple_of(at, block), block)]
                turned[i, c * block : (c + 1) * block, :] = columns.T

    at = 0
    for i, right in enumerate(rights):
        width = right.shape[2]
        value = mm(turned[i], right[0], NN).astype(LOW)
        out_ref[0, :, :, at : at + width] = value.reshape(CELLS // 2, block, width)
        at += width


def weight_grads(lefts, rights, relative, shards, other_core):
    rows, model = lefts[0].shape
    count, block = len(shards), model // CELLS
    width = sum(right.shape[2] for right in rights)

    def right_at(flag):
        def at(s, mp):
            shard = s + shards[0]
            return (jnp.bitwise_xor(shard, mp[0]) if flag else shard), 0, 0

        return at

    return pl.pallas_call(
        lambda mp, *refs: weight_grads_kernel(*refs, other_core=other_core),
        grid_spec=pltpu.PrefetchScalarGridSpec(
            num_scalar_prefetch=1,
            grid=(count,),
            in_specs=[pl.BlockSpec((rows, model), lambda s, mp: (0, 0))] * len(lefts)
            + [
                pl.BlockSpec((1, rows, right.shape[2]), right_at(flag))
                for right, flag in zip(rights, relative)
            ],
            out_specs=pl.BlockSpec((1, CELLS // 2, block, width), lambda s, mp: (s, 0, 0, 0)),
            scratch_shapes=[pltpu.VMEM((len(lefts), model // 2, rows), LOW)],
        ),
        out_shape=jax.ShapeDtypeStruct((count, CELLS // 2, block, width), LOW),
        compiler_params=pltpu.CompilerParams(vmem_limit_bytes=VMEM_LIMIT),
        cost_estimate=pl.CostEstimate(
            flops=rows * model * width * count,
            bytes_accessed=count * model * width,
            transcendentals=0,
        ),
        name="weight_grads",
    )(lax.axis_index("mp").astype(jnp.int32).reshape(1), *lefts, *rights)


def pass_kernel(*refs):
    del refs


def after(values, *others):
    keep = pl.BlockSpec(memory_space=pl.ANY)
    count = len(values)
    return pl.pallas_call(
        pass_kernel,
        in_specs=[keep] * (count + len(others)),
        out_specs=[keep] * count,
        out_shape=[jax.ShapeDtypeStruct(v.shape, v.dtype) for v in values],
        input_output_aliases={i: i for i in range(count)},
        cost_estimate=pl.CostEstimate(flops=0, bytes_accessed=0, transcendentals=0),
        name="order",
    )(*values, *others)


class Layout:
    def __init__(self, dp, mp):
        self.dp, self.mp = dp, mp

    def permute(self, value, move):
        pairs = []
        for d in range(self.dp):
            for m in range(self.mp):
                to_d, to_m = move(d, m)
                pairs.append((d * self.mp + m, to_d * self.mp + to_m))
        return lax.ppermute(value, ("dp", "mp"), pairs)

    def flip(self, value, bits):
        return self.permute(value, lambda d, m: (d ^ bits, m))

    def flip_mp(self, value, bits):
        return self.permute(value, lambda d, m: (d, m ^ bits))

    def cell(self):
        return lax.rem(lax.axis_index("dp"), CELLS)

    def swap_mp(self, blocks):
        return [b if k == 0 else self.flip_mp(b, k) for k, b in enumerate(blocks)]

    def rows_for(self, value):
        rows = value.shape[0] // self.mp
        me = lax.axis_index("mp")
        return [
            lax.dynamic_slice_in_dim(value, jnp.bitwise_xor(me, k) * rows, rows, 0)
            for k in range(self.mp)
        ]

    def in_order(self, blocks):
        rows = blocks[0].shape[0]
        me = lax.axis_index("mp")
        out = jnp.zeros((rows * self.mp,) + blocks[0].shape[1:], blocks[0].dtype)
        for k, b in enumerate(blocks):
            out = lax.dynamic_update_slice_in_dim(out, b, jnp.bitwise_xor(me, k) * rows, 0)
        return out

    def piece(self, slab):
        rows = slab.shape[0] // CELLS
        return lax.dynamic_slice_in_dim(slab, self.cell() * rows, rows, 0)

    def near(self, here, bit):
        return jnp.stack([here, self.flip(here, bit)])

    def core_halves(self, left):
        rows = left.shape[1] // CELLS
        cell = self.cell()
        parts = [
            lax.dynamic_slice_in_dim(left, jnp.bitwise_xor(cell, j) * rows, rows, 1)
            for j in range(CELLS)
        ]
        return jnp.concatenate(parts[0::2], axis=1), jnp.concatenate(parts[1::2], axis=1)

    def fold(self, value, got):
        return (value.astype(WIDE) + got.astype(WIDE)).astype(LOW)

    def chip_halves(self, value, bit):
        count, width = value.shape[0], value.shape[-1]
        value = value.reshape(count, 2, 2, -1, width)
        if bit == 2:
            return value[:, :, 0], value[:, :, 1]
        return value[:, 0], value[:, 1]

    def last_halves(self, value):
        return value[:, 0], value[:, 1]

    def to_rows(self, mine):
        groups = self.dp // CELLS
        if groups == 1:
            return mine
        mine = lax.psum_scatter(
            mine,
            "dp",
            scatter_dimension=1,
            tiled=True,
            axis_index_groups=[[g * CELLS + c for g in range(groups)] for c in range(CELLS)],
        )
        return self.permute(mine, lambda d, m: ((d % CELLS) * groups + d // CELLS, m))

    def sum_all(self, value):
        step = 1
        while step < self.dp:
            value = value + self.flip(value, step)
            step *= 2
        step = 1
        while step < self.mp:
            value = value + self.flip_mp(value, step)
            step *= 2
        return value


def local(
    layout,
    tokens,
    memory,
    self_qkv,
    self_out,
    cross_q,
    cross_kv,
    cross_out,
    ffn_in,
    ffn_out,
    ln_gain,
    ln_bias,
    cotangent,
):
    model_width = tokens.shape[2]
    w = self_out.shape[1]
    n = layout.mp
    tokens, memory, cotangent = (
        v.reshape(v.shape[0], model_width) for v in (tokens, memory, cotangent)
    )
    rows = tokens.shape[0]
    qkv_flat = self_qkv.reshape(model_width, 3 * w)
    kv_flat = cross_kv.reshape(model_width, 2 * w)
    n_hidden = ffn_in.shape[1]
    half = n // 2
    pieces = [layout.piece(v) for v in (self_out, cross_q, ffn_in, ffn_out, cross_out)]
    weights = lax.all_gather(jnp.concatenate(pieces, axis=1), "mp", axis=0, tiled=False)
    (tokens_there,) = after([tokens], weights)
    full_tokens = lax.all_gather(tokens_there, "mp", axis=0, tiled=True)
    attn_here = layout.near(weights[:, :, : 2 * w], 2)
    ffn_own = after(
        [weights[h * half : (h + 1) * half, :, 2 * w :] for h in range(2)], attn_here
    )
    attn_there = layout.flip(attn_here, 4)
    ffn_here = [layout.near(part, bit) for part, bit in zip(ffn_own, BITS)]
    full_tokens, *ffn_here = after([full_tokens, *ffn_here], weights)
    (memory_there,) = after([memory], full_tokens)
    full_memory = lax.all_gather(memory_there, "mp", axis=0, tiled=True)

    projected = dense(full_tokens, qkv_flat).astype(LOW)
    pairs = w // (2 * HD)
    self_operands = (projected, 0), (projected, pairs), (projected, 2 * pairs)
    home_attended, self_logs = attend(w, *self_operands, True, *SELF_BLOCKS)
    attended_blocks = layout.swap_mp(layout.rows_for(home_attended))
    attn_here, attn_there = after([attn_here, attn_there], home_attended)
    ffn_there = [layout.flip(part, 6 - bit) for part, bit in zip(ffn_here, BITS)]
    attn_parts = [attn_here, attn_there, layout.flip(attn_here, 1), layout.flip(attn_there, 1)]
    first_n, first_scale, first_low, *query_blocks = enter_cross(
        tokens, ln_gain, ln_bias, attended_blocks, attn_parts
    )
    query_blocks = layout.swap_mp(query_blocks)
    cross_queries = jnp.concatenate(query_blocks)
    ffn_here_other = [layout.flip(part, 1) for part in ffn_here]
    cross_pair = dense(full_memory, kv_flat).astype(LOW)
    cross_operands = (cross_queries, 0), (cross_pair, 0), (cross_pair, pairs)
    home_cross, cross_logs = attend(w, *cross_operands, False, *CROSS_BLOCKS)
    ffn_there = after(ffn_there, home_cross)
    ffn_there_other = [layout.flip(part, 1) for part in ffn_there]
    ffn_parts = list(zip(ffn_here, ffn_there, ffn_here_other, ffn_there_other))
    cross_blocks = layout.swap_mp(list(home_cross.reshape(n, rows, w)))
    (
        mixed,
        second_low,
        third_low,
        cross_grad,
        cross_grad_low,
        later_terms,
        activation,
        hidden_grad,
        *cross_grad_blocks,
    ) = feed_forward(
        first_n, cotangent, ln_gain, ln_bias, cross_blocks, n_hidden, ffn_parts
    )
    cross_grad_blocks = layout.swap_mp(cross_grad_blocks)
    cross_attended = jnp.stack(cross_blocks)

    def fold_chip(pair, bit):
        return layout.chip_halves(layout.fold(*pair), bit)

    def send(pair, bit):
        return pair[0], layout.flip(pair[1], bit)

    def fold_last(pair):
        return layout.last_halves(layout.fold(*pair))

    ffn_grads = functools.partial(
        weight_grads,
        [second_low, third_low, cross_grad_low],
        [hidden_grad, activation, cross_attended],
        [False, False, True],
    )
    cuts = (range(0, half), range(half, n))
    ffn_sums = [send((None, ffn_grads(cut, 1)), 1)[1] for cut in cuts]
    ffn_sums = [(ffn_grads(cut, 0), got) for cut, got in zip(cuts, ffn_sums)]
    (cross_attended_grad,) = after(
        [jnp.concatenate(cross_grad_blocks)], *(here for here, _ in ffn_sums)
    )
    cross_queries_grad, cross_keys_grad, cross_values_grad = attend_back(
        w, *cross_operands, cross_attended_grad, home_cross, cross_logs, False, *CROSS_BACK_BLOCKS
    )
    first_terms = layout.swap_mp(list(cross_queries_grad.reshape(n, rows, w)))
    cross_pair_grad = jnp.concatenate([cross_keys_grad, cross_values_grad], axis=-1)
    memory_term = back_dense(cross_pair_grad, kv_flat).astype(LOW)
    memory_grad = lax.psum_scatter(memory_term, "mp", scatter_dimension=0, tiled=True)
    ffn_sums = [fold_chip(pair, bit) for pair, bit in zip(ffn_sums, BITS)]
    first_terms[1:] = after(first_terms[1:], memory_term, *(there for _, there in ffn_sums))
    ffn_sums = [send(pair, bit) for pair, bit in zip(ffn_sums, BITS)]
    self_grad, self_grad_low, first_norm_terms, *attended_grad_blocks = leave_cross(
        cross_grad, ln_gain, first_n, first_scale, first_terms, attn_parts
    )
    attended_grad = layout.in_order(layout.swap_mp(attended_grad_blocks))
    attn_grads = functools.partial(
        weight_grads,
        [self_grad_low, first_low],
        [jnp.stack(attended_blocks), jnp.stack(first_terms)],
        [True, True],
        range(n),
    )
    attn_here, attn_there = attn_grads(0), attn_grads(1)
    (attended_grad,) = after([attended_grad], attn_here, attn_there, memory_grad)
    attn_sum = attn_here, layout.flip(attn_there, 1)
    queries_grad, keys_grad, values_grad = attend_back(
        w, *self_operands, attended_grad, home_attended, self_logs, True, *SELF_BACK_BLOCKS
    )
    projected_grad = jnp.concatenate([queries_grad, keys_grad, values_grad], axis=-1)
    token_term = back_dense(projected_grad, qkv_flat).astype(LOW)
    token_part = lax.psum_scatter(token_term, "mp", scatter_dimension=0, tiled=True)
    token_grad = (alpha_scale * self_grad + token_part.astype(WIDE)).astype(LOW)
    home_grads = [
        jnp.concatenate(
            [weight_grad(a, cross_pair_grad), weight_grad(b, projected_grad)], axis=1
        )[None]
        for a, b in zip(layout.core_halves(full_memory), layout.core_halves(full_tokens))
    ]
    ffn_sums = [fold_last(pair) for pair in ffn_sums]
    ffn_sums = [send(pair, 6 - bit) for pair, bit in zip(ffn_sums, BITS)]
    attn_sum = send(fold_chip(attn_sum, 2), 2)
    home_sum = send(fold_chip((home_grads[0], layout.flip(home_grads[1], 1)), 4), 4)
    attn_sum = send(fold_last(attn_sum), 4)
    home_sum = send(fold_last(home_sum), 2)
    ffn_sums = jnp.concatenate([layout.fold(*pair) for pair in ffn_sums])
    shards = jnp.concatenate([layout.fold(*attn_sum), ffn_sums], axis=2)
    shard = lax.psum_scatter(shards, "mp", scatter_dimension=0, tiled=True)
    shard = layout.to_rows(shard)[0].astype(WIDE)
    home_grad = layout.to_rows(layout.fold(*home_sum))[0].astype(WIDE)
    sums = layout.sum_all(jnp.concatenate([first_norm_terms, later_terms]))
    edges = (w, 2 * w, 2 * w + n_hidden, 2 * w + 2 * n_hidden)
    self_out_grad, cross_q_grad, ffn_in_grad, ffn_out_grad, cross_out_grad = jnp.split(
        shard, edges, axis=1
    )
    return (
        mixed[:, None],
        token_grad[:, None],
        memory_grad[:, None],
        home_grad[:, 2 * w :].reshape(-1, 3, w),
        self_out_grad,
        cross_q_grad,
        home_grad[:, : 2 * w].reshape(-1, 2, w),
        cross_out_grad,
        ffn_in_grad,
        ffn_out_grad,
        sums[0::2],
        sums[1::2],
    )


def solution(mesh):
    layout = Layout(mesh.shape["dp"], mesh.shape["mp"])
    in_specs = (
        P("mp", "dp", None),
        P("mp", "dp", None),
        P(None, None, "mp"),
        P(None, "mp"),
        P(None, "mp"),
        P(None, None, "mp"),
        P(None, "mp"),
        P(None, "mp"),
        P(None, "mp"),
        P(),
        P(),
        P("mp", "dp", None),
    )
    out_specs = (
        P("mp", "dp", None),
        P("mp", "dp", None),
        P("mp", "dp", None),
        P("dp", None, "mp"),
        P("dp", "mp"),
        P("dp", "mp"),
        P("dp", None, "mp"),
        P("dp", "mp"),
        P("dp", "mp"),
        P("dp", "mp"),
        P(),
        P(),
    )

    def whole(*arrays):
        return local(layout, *arrays)

    return jax.shard_map(whole, mesh=mesh, in_specs=in_specs, out_specs=out_specs, check_vma=False)
```

```python
import functools
import math

import jax
import jax.numpy as jnp
from jax import lax
from jax.experimental import pallas as pl
from jax.experimental.pallas import tpu as pltpu
from jax.sharding import PartitionSpec as P

HD = 64
CELLS = 8
BITS = (2, 4)
LOW = jnp.bfloat16
WIDE = jnp.float32
SELF_BLOCKS = (512, 512)
CROSS_BLOCKS = (1024, 256)
SELF_BACK_BLOCKS = (512, 512)
CROSS_BACK_BLOCKS = (1024, 256)
VMEM_LIMIT = 56 * 2**20

alpha_scale = 300.0**0.25
norm_eps = 1e-05

NN = (((1,), (0,)), ((), ()))
NT = (((1,), (1,)), ((), ()))
TN = (((0,), (0,)), ((), ()))


def dense(left, weight):
    return jnp.einsum("td,df->tf", left, weight, preferred_element_type=WIDE)


def weight_grad(left, grad):
    return jnp.einsum("td,tf->df", left, grad, preferred_element_type=WIDE).astype(LOW)


def back_dense(grad, weight):
    return jnp.einsum("tf,df->td", grad, weight, preferred_element_type=WIDE)


def mm(left, right, dims):
    return lax.dot_general(left, right, dims, preferred_element_type=WIDE)


def keep_head(value, head):
    at = lax.broadcasted_iota(jnp.int32, value.shape, 1) // HD
    return jnp.where(at == head, value, jnp.zeros_like(value))


def masked(scores, key_begin, query_begin):
    key_at = lax.broadcasted_iota(jnp.int32, scores.shape, 0) + key_begin
    query_at = lax.broadcasted_iota(jnp.int32, scores.shape, 1) + query_begin
    return jnp.where(key_at <= query_at, scores, -1000000000.0)


def key_blocks(body, carry, query_block, key_block, keys, causal):
    if not causal:
        for j in range(keys // key_block):
            carry = body(j, carry, False)
        return carry
    per = query_block // key_block
    begin = pl.program_id(1) * per
    carry = lax.fori_loop(0, begin, lambda j, c: body(j, c, False), carry)
    for e in range(per):
        carry = body(begin + e, carry, True)
    return carry


def attend_kernel(q_ref, k_ref, v_ref, o_ref, lse_ref, *, key_block, causal):
    query_block = q_ref.shape[0]
    query_begin = pl.program_id(1) * query_block
    q = q_ref[...] * jnp.asarray(1.0 / math.sqrt(HD), LOW)

    def body(j, carry, diagonal):
        tops, sums, acc = carry[:2], carry[2:4], carry[4]
        at = pl.multiple_of(j * key_block, key_block)
        k, v = k_ref[pl.ds(at, key_block), :], v_ref[pl.ds(at, key_block), :]
        new_tops, new_sums, shrink, parts = [], [], [], []
        for head in (0, 1):
            s = mm(keep_head(k, head), q, NT)
            if diagonal:
                s = masked(s, j * key_block, query_begin)
            top = jnp.maximum(tops[head], jnp.max(s, axis=0, keepdims=True))
            p = jnp.exp(s - top)
            factor = jnp.exp(tops[head] - top)
            new_tops.append(top)
            new_sums.append(sums[head] * factor + jnp.sum(p, axis=0, keepdims=True))
            shrink.append(factor)
            parts.append(mm(keep_head(v, head), p.astype(LOW), TN))
        upper = lax.broadcasted_iota(jnp.int32, acc.shape, 0) < HD
        acc = acc * jnp.where(upper, shrink[0], shrink[1]) + (parts[0] + parts[1])
        return (*new_tops, *new_sums, acc)

    low = jnp.full((1, query_block), -1e30, WIDE)
    zero = jnp.zeros((1, query_block), WIDE)
    start = (low, low, zero, zero, jnp.zeros((2 * HD, query_block), WIDE))
    top0, top1, sum0, sum1, acc = key_blocks(
        body, start, query_block, key_block, k_ref.shape[0], causal
    )
    upper = lax.broadcasted_iota(jnp.int32, acc.shape, 0) < HD
    o_ref[...] = (acc * jnp.where(upper, 1.0 / sum0, 1.0 / sum1)).T.astype(LOW)
    lse_ref[0] = jnp.concatenate(
        [top0 + jnp.log(sum0), top1 + jnp.log(sum1), jnp.zeros((6, query_block), WIDE)], axis=0
    )


def attend_back_kernel(
    q_ref, g_ref, o_ref, lse_ref, k_ref, v_ref, dq_ref, dk_ref, dv_ref, dk_acc, dv_acc, *, key_block, causal
):
    query_block = q_ref.shape[0]
    query_begin = pl.program_id(1) * query_block

    @pl.when(pl.program_id(1) == 0)
    def _():
        dk_acc[...] = jnp.zeros_like(dk_acc)
        dv_acc[...] = jnp.zeros_like(dv_acc)

    q = q_ref[...] * jnp.asarray(1.0 / math.sqrt(HD), LOW)
    g = g_ref[...]
    q_heads = [keep_head(q, head) for head in (0, 1)]
    g_heads = [keep_head(g, head) for head in (0, 1)]
    picks = lax.broadcasted_iota(jnp.int32, (8, 2 * HD), 1) // HD
    picks = (picks == lax.broadcasted_iota(jnp.int32, (8, 2 * HD), 0)).astype(WIDE)
    inner = lax.dot_general(
        picks,
        g.astype(WIDE) * o_ref[...].astype(WIDE),
        NT,
        precision=lax.Precision.HIGHEST,
        preferred_element_type=WIDE,
    )
    lse = lse_ref[0]

    def body(j, dq, diagonal):
        at = pl.multiple_of(j * key_block, key_block)
        k, v = k_ref[pl.ds(at, key_block), :], v_ref[pl.ds(at, key_block), :]
        dk, dv = dk_acc[pl.ds(at, key_block), :], dv_acc[pl.ds(at, key_block), :]
        for head in (0, 1):
            k_head = keep_head(k, head)
            s = mm(k_head, q, NT)
            if diagonal:
                s = masked(s, j * key_block, query_begin)
            p = jnp.exp(s - lse[head : head + 1])
            dp = mm(keep_head(v, head), g, NT)
            ds = (p * (dp - inner[head : head + 1])).astype(LOW)
            dv = dv + mm(p.astype(LOW), g_heads[head], NN)
            dk = dk + mm(ds, q_heads[head], NN)
            dq = dq + mm(k_head, ds, TN)
        dk_acc[pl.ds(at, key_block), :] = dk
        dv_acc[pl.ds(at, key_block), :] = dv
        return dq

    dq = key_blocks(
        body, jnp.zeros((2 * HD, query_block), WIDE), query_block, key_block, k_ref.shape[0], causal
    )
    dq_ref[...] = (dq * (1.0 / math.sqrt(HD))).T.astype(LOW)

    @pl.when(pl.program_id(1) == pl.num_programs(1) - 1)
    def _():
        dk_ref[...] = dk_acc[...].astype(LOW)
        dv_ref[...] = dv_acc[...].astype(LOW)


def columns_of(rows, first, whole):
    if whole:
        return pl.BlockSpec((rows, 2 * HD), lambda p, i: (0, first + p))
    return pl.BlockSpec((rows, 2 * HD), lambda p, i: (i, first + p))


def attend(width, queries, keys, values, causal, query_block, key_block):
    seq, span = queries[0].shape[0], keys[0].shape[0]
    pairs = width // (2 * HD)
    return pl.pallas_call(
        functools.partial(attend_kernel, key_block=key_block, causal=causal),
        grid=(pairs, seq // query_block),
        in_specs=[
            columns_of(query_block, queries[1], False),
            columns_of(span, keys[1], True),
            columns_of(span, values[1], True),
        ],
        out_specs=[
            columns_of(query_block, 0, False),
            pl.BlockSpec((1, 8, query_block), lambda p, i: (p, 0, i)),
        ],
        out_shape=[
            jax.ShapeDtypeStruct((seq, width), LOW),
            jax.ShapeDtypeStruct((pairs, 8, seq), WIDE),
        ],
        compiler_params=pltpu.CompilerParams(vmem_limit_bytes=VMEM_LIMIT),
        cost_estimate=pl.CostEstimate(
            flops=8 * seq * span * width, bytes_accessed=8 * seq * width, transcendentals=0
        ),
        name="attend",
    )(queries[0], keys[0], values[0])


def attend_back(width, queries, keys, values, grad, result, lse, causal, query_block, key_block):
    seq, span = queries[0].shape[0], keys[0].shape[0]
    pairs = width // (2 * HD)
    whole = columns_of(span, 0, True)
    return pl.pallas_call(
        functools.partial(attend_back_kernel, key_block=key_block, causal=causal),
        grid=(pairs, seq // query_block),
        in_specs=[
            columns_of(query_block, queries[1], False),
            columns_of(query_block, 0, False),
            columns_of(query_block, 0, False),
            pl.BlockSpec((1, 8, query_block), lambda p, i: (p, 0, i)),
            columns_of(span, keys[1], True),
            columns_of(span, values[1], True),
        ],
        out_specs=[columns_of(query_block, 0, False), whole, whole],
        out_shape=[
            jax.ShapeDtypeStruct((seq, width), LOW),
            jax.ShapeDtypeStruct((span, width), LOW),
            jax.ShapeDtypeStruct((span, width), LOW),
        ],
        scratch_shapes=[pltpu.VMEM((span, 2 * HD), WIDE), pltpu.VMEM((span, 2 * HD), WIDE)],
        compiler_params=pltpu.CompilerParams(vmem_limit_bytes=VMEM_LIMIT),
        cost_estimate=pl.CostEstimate(
            flops=16 * seq * span * width, bytes_accessed=16 * seq * width, transcendentals=0
        ),
        name="attend_back",
    )(queries[0], grad, result, lse, keys[0], values[0])


def normalized(value):
    center = value - jnp.mean(value, axis=-1, keepdims=True)
    scale = lax.rsqrt(jnp.mean(center * center, axis=-1, keepdims=True) + norm_eps)
    return center * scale, scale


def norm_back(grad, gain, n, scale):
    e = grad * gain
    mean_e = jnp.mean(e, axis=-1, keepdims=True)
    mean_en = jnp.mean(e * n, axis=-1, keepdims=True)
    terms = jnp.concatenate(
        [jnp.sum(grad * n, axis=0, keepdims=True), jnp.sum(grad, axis=0, keepdims=True)], axis=0
    )
    return (e - mean_e - n * mean_en) * scale, terms


def gelu_with_slope(value):
    c = math.sqrt(2.0 / math.pi)
    square = value * value
    t = jnp.tanh(c * value * (1.0 + 0.044715 * square))
    half = 0.5 * (1.0 + t)
    slope = half + 0.5 * value * (1.0 - t * t) * (c * (1.0 + 3 * 0.044715 * square))
    return value * half, slope


def cell_copies(parts, first, target, sems, pick):
    cell = lax.rem(lax.axis_index("dp"), CELLS)
    rows = target.shape[-2] // CELLS
    copies = []
    for j in range(CELLS):
        part = parts[(j & 1) * 2 + (1 if j & (6 - first) else 0)].at[1 if j & first else 0]
        at = pl.multiple_of(jnp.bitwise_xor(cell, j) * rows, rows)
        copies.append(pltpu.make_async_copy(*pick(part, target, pl.ds(at, rows)), sems.at[j]))
    return copies


def attention_copies(own, parts, weights, sems, width):
    count = weights.shape[0]
    copies = [
        pltpu.make_async_copy(own[0], weights.at[0, :, :width], sems.at[CELLS]),
        pltpu.make_async_copy(own[1], weights.at[0, :, width:], sems.at[CELLS + 1]),
    ]
    return copies + cell_copies(
        parts, 2, weights, sems, lambda part, to, at: (part, to.at[pl.ds(1, count - 1), at, :])
    )


def start_all(copies):
    for copy in copies:
        copy.start()


def wait_all(copies):
    for copy in copies:
        copy.wait()


def enter_cross_kernel(
    tokens_ref, gain_ref, bias_ref, *refs, width, count
):
    attended, refs = refs[:count], refs[count:]
    own, parts, refs = refs[:2], refs[2:6], refs[6:]
    n_ref, scale_ref, low_ref = refs[:3]
    queries, (weights, sems) = refs[3 : 3 + count], refs[3 + count :]
    copies = attention_copies(own, parts, weights, sems, width)
    start_all(copies)
    value = alpha_scale * tokens_ref[...].astype(WIDE)
    wait_all(copies)
    for k in range(count):
        value = value + mm(attended[k][...], weights[k, :, :width], NT)
    n, scale = normalized(value)
    n_ref[...] = n
    scale_ref[...] = jnp.broadcast_to(scale, scale_ref.shape)
    low = (n * gain_ref[0:1, :] + bias_ref[0:1, :]).astype(LOW)
    low_ref[...] = low
    for k in range(count):
        queries[k][...] = mm(low, weights[k, :, width:], NN).astype(LOW)


def leave_cross_kernel(
    cross_grad_ref, gain_ref, n_ref, scale_ref, *refs, width, count
):
    queries, refs = refs[:count], refs[count:]
    own, parts, refs = refs[:2], refs[2:6], refs[6:]
    self_grad_ref, low_ref, terms_ref = refs[:3]
    grads, (weights, sems) = refs[3 : 3 + count], refs[3 + count :]
    copies = attention_copies(own, parts, weights, sems, width)
    start_all(copies)
    grad = alpha_scale * cross_grad_ref[...]
    wait_all(copies)
    for k in range(count):
        grad = grad + mm(queries[k][...], weights[k, :, width:], NT)
    self_grad, terms_ref[...] = norm_back(grad, gain_ref[0:1, :], n_ref[...], scale_ref[:, :1])
    self_grad_ref[...] = self_grad
    low = self_grad.astype(LOW)
    low_ref[...] = low
    for k in range(count):
        grads[k][...] = mm(low, weights[k, :, :width], NN).astype(LOW)


def feed_forward_kernel(
    first_n_ref, cotangent_ref, gain_ref, bias_ref, *refs, width, count
):
    attended, refs = refs[:count], refs[count:]
    own, in_parts, out_parts, refs = refs[:3], refs[3:7], refs[7:11], refs[11:]
    mixed_ref, second_low_ref, third_low_ref, cross_grad_ref, cross_low_ref, terms_ref = refs[:6]
    act_ref, hidden_grad_ref = refs[6:8]
    grads, refs = refs[8 : 8 + count], refs[8 + count :]
    w_in, w_out, w_cross, slope_ref, sum_ref, in_sems, out_sems, cross_sems = refs
    hidden = w_in.shape[2]
    chunk = min(512, hidden)

    cross_copies = [pltpu.make_async_copy(own[2], w_cross.at[0], cross_sems.at[CELLS])]
    cross_copies += cell_copies(
        out_parts,
        4,
        w_cross,
        cross_sems,
        lambda part, to, at: (part.at[:, :, hidden:], to.at[pl.ds(1, count - 1), at, :]),
    )
    start_all(cross_copies)
    in_copies = [[pltpu.make_async_copy(own[0], w_in.at[0], in_sems.at[0, 0])]]
    out_copies = [[pltpu.make_async_copy(own[1], w_out.at[0], out_sems.at[0, 0])]]
    for k in range(1, count):
        in_copies.append(
            cell_copies(
                in_parts,
                2,
                w_in,
                in_sems.at[k],
                lambda part, to, at: (part.at[k - 1], to.at[k, at, :]),
            )
        )
        out_copies.append(
            cell_copies(
                out_parts,
                4,
                w_out,
                out_sems.at[k],
                lambda part, to, at: (part.at[k - 1, :, :hidden], to.at[k, at, :]),
            )
        )
    for copies in zip(in_copies, out_copies):
        start_all(copies[0])
        start_all(copies[1])

    second = alpha_scale * (first_n_ref[...] * gain_ref[0:1, :] + bias_ref[0:1, :])
    wait_all(cross_copies)
    for k in range(count):
        second = second + mm(attended[k][...], w_cross[k], NT)
    second_n, second_scale = normalized(second)
    second = second_n * gain_ref[1:2, :] + bias_ref[1:2, :]
    second_low = second.astype(LOW)
    second_low_ref[...] = second_low
    sum_ref[...] = alpha_scale * second
    for k in range(count):
        wait_all(in_copies[k])
        for begin in range(0, hidden, chunk):
            cut = slice(begin, begin + chunk)
            value = mm(second_low, w_in[k, :, cut], NN)
            act, slope = gelu_with_slope(value)
            slope_ref[k, :, cut] = slope
            act_ref[k, :, cut] = act.astype(LOW)
        wait_all(out_copies[k])
        sum_ref[...] += mm(act_ref[k], w_out[k], NT)
    third_n, third_scale = normalized(sum_ref[...])
    mixed_ref[...] = (third_n * gain_ref[2:3, :] + bias_ref[2:3, :]).astype(LOW)
    third_grad, third_terms = norm_back(
        cotangent_ref[...].astype(WIDE), gain_ref[2:3, :], third_n, third_scale
    )
    third_low = third_grad.astype(LOW)
    third_low_ref[...] = third_low
    sum_ref[...] = alpha_scale * third_grad
    for k in range(count):
        for begin in range(0, hidden, chunk):
            cut = slice(begin, begin + chunk)
            act_grad = mm(third_low, w_out[k, :, cut], NN).astype(LOW).astype(WIDE)
            hidden_grad_ref[k, :, cut] = (act_grad * slope_ref[k, :, cut]).astype(LOW)
        sum_ref[...] += mm(hidden_grad_ref[k], w_in[k], NT)
    cross_grad, second_terms = norm_back(sum_ref[...], gain_ref[1:2, :], second_n, second_scale)
    terms_ref[...] = jnp.concatenate([second_terms, third_terms], axis=0)
    cross_grad_ref[...] = cross_grad
    cross_low = cross_grad.astype(LOW)
    cross_low_ref[...] = cross_low
    for k in range(count):
        grads[k][...] = mm(cross_low, w_cross[k], NN).astype(LOW)


def call(kernel, operands, streamed, results, scratch, flops, name):
    here, there = pl.BlockSpec(memory_space=pltpu.VMEM), pl.BlockSpec(memory_space=pl.ANY)
    arrays = [*operands, *streamed]
    size = sum(v.size * v.dtype.itemsize for v in arrays)
    return pl.pallas_call(
        kernel,
        in_specs=[here] * len(operands) + [there] * len(streamed),
        out_specs=[here] * len(results),
        out_shape=[jax.ShapeDtypeStruct(shape, dtype) for shape, dtype in results],
        scratch_shapes=scratch,
        compiler_params=pltpu.CompilerParams(vmem_limit_bytes=VMEM_LIMIT),
        cost_estimate=pl.CostEstimate(flops=flops, bytes_accessed=size, transcendentals=0),
        name=name,
    )(*arrays)


def project_kernel(*refs, count):
    blocks, (weight_ref, tokens_ref, out_ref) = refs[:count], refs[count:]
    rows = tokens_ref.shape[0] // count
    for k in range(count):
        at = jnp.bitwise_xor(lax.axis_index("mp"), k) * rows
        at = pl.ds(pl.multiple_of(at, rows), rows)
        block = blocks[k][:rows, :]
        tokens_ref[at, :] = block
        out_ref[at, :] = mm(block, weight_ref[...], NN).astype(LOW)


def project(blocks, rows, weight):
    count, model = len(blocks), blocks[0].shape[1]
    return call(
        functools.partial(project_kernel, count=count),
        [*blocks, weight],
        [],
        [((count * rows, model), LOW), ((count * rows, weight.shape[1]), LOW)],
        [],
        2 * count * rows * model * weight.shape[1],
        "project",
    )


def enter_cross(tokens, gain, bias, attended, own, parts):
    rows, model = tokens.shape
    count, width = len(attended), attended[0].shape[1]
    return call(
        functools.partial(enter_cross_kernel, width=width, count=count),
        [tokens, gain, bias, *attended],
        [*own, *parts],
        [((rows, model), WIDE), ((rows, 128), WIDE), ((rows, model), LOW)]
        + [((rows, width), LOW)] * count,
        [
            pltpu.VMEM((count, model, 2 * width), LOW),
            pltpu.SemaphoreType.DMA((CELLS + 2,)),
        ],
        4 * rows * model * width * count,
        "enter_cross",
    )


def leave_cross(cross_grad, gain, n, scale, queries, own, parts):
    rows, model = n.shape
    count, width = len(queries), queries[0].shape[1]
    return call(
        functools.partial(leave_cross_kernel, width=width, count=count),
        [cross_grad, gain, n, scale, *queries],
        [*own, *parts],
        [((rows, model), WIDE), ((rows, model), LOW), ((2, model), WIDE)]
        + [((rows, width), LOW)] * count,
        [
            pltpu.VMEM((count, model, 2 * width), LOW),
            pltpu.SemaphoreType.DMA((CELLS + 2,)),
        ],
        4 * rows * model * width * count,
        "leave_cross",
    )


def feed_forward(first_n, cotangent, gain, bias, attended, own, in_parts, out_parts):
    rows, model = first_n.shape
    count, width = len(attended), attended[0].shape[1]
    hidden = own[0].shape[1]
    sems = pltpu.SemaphoreType.DMA((count, CELLS))
    return call(
        functools.partial(feed_forward_kernel, width=width, count=count),
        [first_n, cotangent, gain, bias, *attended],
        [*own, *in_parts, *out_parts],
        [
            ((rows, model), LOW),
            ((rows, model), LOW),
            ((rows, model), LOW),
            ((rows, model), WIDE),
            ((rows, model), LOW),
            ((4, model), WIDE),
            ((count, rows, hidden), LOW),
            ((count, rows, hidden), LOW),
        ]
        + [((rows, width), LOW)] * count,
        [
            pltpu.VMEM((count, model, hidden), LOW),
            pltpu.VMEM((count, model, hidden), LOW),
            pltpu.VMEM((count, model, width), LOW),
            pltpu.VMEM((count, rows, hidden), WIDE),
            pltpu.VMEM((rows, model), WIDE),
            sems,
            sems,
            pltpu.SemaphoreType.DMA((CELLS + 1,)),
        ],
        8 * rows * model * hidden * count,
        "feed_forward",
    )


def chip_cells(bit):
    keep = [c for c in range(CELLS // 2) if not (2 * c) & bit]
    return keep, [c for c in range(CELLS // 2) if (2 * c) & bit]


def weight_grads_kernel(*refs, count, other_core, bit):
    lefts, rights, refs = refs[:count], refs[count : 2 * count], refs[2 * count :]
    turned = refs[-1]
    block = turned.shape[1] // (CELLS // 2)

    @pl.when(pl.program_id(0) == 0)
    def _():
        cell = lax.rem(lax.axis_index("dp"), CELLS)
        for i, left in enumerate(lefts):
            for c in range(CELLS // 2):
                at = jnp.bitwise_xor(cell, 2 * c + other_core) * block
                columns = left[:, pl.ds(pl.multiple_of(at, block), block)]
                turned[i, c * block : (c + 1) * block, :] = columns.T

    at = 0
    for i, right in enumerate(rights):
        cut = slice(at, at + right.shape[2])
        at += right.shape[2]
        value = mm(turned[i], right[0], NN).reshape(CELLS // 2, block, right.shape[2])
        if bit is None:
            refs[0][:, 0, :, cut] = value.astype(LOW)
            continue
        got, *outs = refs[:3]
        for out, cells in zip(outs, chip_cells(bit)):
            for e, c in enumerate(cells):
                out[e, 0, :, cut] = (value[c] + got[c, 0, :, cut].astype(WIDE)).astype(LOW)


def weight_grads(lefts, rights, shards, other_core, got=None, bit=None):
    rows, model = lefts[0].shape
    count, block, cells = len(shards), model // CELLS, CELLS // 2
    width = sum(right.shape[2] for right in rights)

    def right_at(s, mp):
        return jnp.bitwise_xor(s + shards[0], mp[0]), 0, 0

    def whole(cells):
        return pl.BlockSpec((cells, 1, block, width), lambda s, mp: (0, s, 0, 0))

    def result(cells):
        return jax.ShapeDtypeStruct((cells, count, block, width), LOW)

    halves = got is not None
    kernel = functools.partial(
        weight_grads_kernel, count=len(lefts), other_core=other_core, bit=bit
    )
    return pl.pallas_call(
        lambda mp, *refs: kernel(*refs),
        grid_spec=pltpu.PrefetchScalarGridSpec(
            num_scalar_prefetch=1,
            grid=(count,),
            in_specs=[pl.BlockSpec((rows, model), lambda s, mp: (0, 0))] * len(lefts)
            + [pl.BlockSpec((1, rows, right.shape[2]), right_at) for right in rights]
            + [whole(cells)] * halves,
            out_specs=[whole(cells // 2)] * 2 if halves else whole(cells),
            scratch_shapes=[pltpu.VMEM((len(lefts), model // 2, rows), LOW)],
        ),
        out_shape=[result(cells // 2)] * 2 if halves else result(cells),
        compiler_params=pltpu.CompilerParams(vmem_limit_bytes=VMEM_LIMIT),
        cost_estimate=pl.CostEstimate(
            flops=rows * model * width * count,
            bytes_accessed=count * model * width,
            transcendentals=0,
        ),
        name="weight_grads",
    )(
        lax.axis_index("mp").astype(jnp.int32).reshape(1),
        *lefts,
        *rights,
        *([got] if halves else []),
    )


def pass_kernel(*refs):
    del refs


def after(values, *others):
    keep = pl.BlockSpec(memory_space=pl.ANY)
    count = len(values)
    return pl.pallas_call(
        pass_kernel,
        in_specs=[keep] * (count + len(others)),
        out_specs=[keep] * count,
        out_shape=[jax.ShapeDtypeStruct(v.shape, v.dtype) for v in values],
        input_output_aliases={i: i for i in range(count)},
        cost_estimate=pl.CostEstimate(flops=0, bytes_accessed=0, transcendentals=0),
        name="order",
    )(*values, *others)


class Layout:
    def __init__(self, dp, mp):
        self.dp, self.mp = dp, mp

    def permute(self, value, move):
        pairs = []
        for d in range(self.dp):
            for m in range(self.mp):
                to_d, to_m = move(d, m)
                pairs.append((d * self.mp + m, to_d * self.mp + to_m))
        return lax.ppermute(value, ("dp", "mp"), pairs)

    def flip(self, value, bits):
        return self.permute(value, lambda d, m: (d ^ bits, m))

    def flip_mp(self, value, bits):
        return self.permute(value, lambda d, m: (d, m ^ bits))

    def cell(self):
        return lax.rem(lax.axis_index("dp"), CELLS)

    def swap_mp(self, blocks):
        return [b if k == 0 else self.flip_mp(b, k) for k, b in enumerate(blocks)]

    def rows_for(self, value):
        rows = value.shape[0] // self.mp
        me = lax.axis_index("mp")
        return [
            lax.dynamic_slice_in_dim(value, jnp.bitwise_xor(me, k) * rows, rows, 0)
            for k in range(self.mp)
        ]

    def in_order(self, blocks):
        rows = blocks[0].shape[0]
        me = lax.axis_index("mp")
        out = jnp.zeros((rows * self.mp,) + blocks[0].shape[1:], blocks[0].dtype)
        for k, b in enumerate(blocks):
            out = lax.dynamic_update_slice_in_dim(out, b, jnp.bitwise_xor(me, k) * rows, 0)
        return out

    def piece(self, slab):
        rows = slab.shape[0] // CELLS
        return lax.dynamic_slice_in_dim(slab, self.cell() * rows, rows, 0)

    def near(self, here, bit):
        return jnp.stack([here, self.flip(here, bit)])

    def core_halves(self, left):
        rows = left.shape[1] // CELLS
        cell = self.cell()
        parts = [
            lax.dynamic_slice_in_dim(left, jnp.bitwise_xor(cell, j) * rows, rows, 1)
            for j in range(CELLS)
        ]
        return jnp.concatenate(parts[0::2], axis=1), jnp.concatenate(parts[1::2], axis=1)

    def fold(self, value, got):
        return (value.astype(WIDE) + got.astype(WIDE)).astype(LOW)

    def to_rows(self, mine):
        groups = self.dp // CELLS
        if groups == 1:
            return mine
        mine = lax.psum_scatter(
            mine,
            "dp",
            scatter_dimension=1,
            tiled=True,
            axis_index_groups=[[g * CELLS + c for g in range(groups)] for c in range(CELLS)],
        )
        return self.permute(mine, lambda d, m: ((d % CELLS) * groups + d // CELLS, m))

    def sum_dp(self, value):
        step = 1
        while step < self.dp:
            value = value + self.flip(value, step)
            step *= 2
        return value


def local(
    layout,
    tokens,
    memory,
    self_qkv,
    self_out,
    cross_q,
    cross_kv,
    cross_out,
    ffn_in,
    ffn_out,
    ln_gain,
    ln_bias,
    cotangent,
):
    model_width = tokens.shape[2]
    w = self_out.shape[1]
    n = layout.mp
    tokens, memory, cotangent = (
        v.reshape(v.shape[0], model_width) for v in (tokens, memory, cotangent)
    )
    rows = tokens.shape[0]
    qkv_flat = self_qkv.reshape(model_width, 3 * w)
    kv_flat = cross_kv.reshape(model_width, 2 * w)
    n_hidden = ffn_in.shape[1]
    half = n // 2
    order = [jnp.bitwise_xor(lax.axis_index("mp"), k) for k in range(n)]

    full_tokens = lax.all_gather(tokens, "mp", axis=0, tiled=True)
    pieces = [layout.piece(v) for v in (self_out, cross_q, ffn_in, ffn_out, cross_out)]
    attn_here = jnp.stack(layout.swap_mp([jnp.concatenate(pieces[:2], axis=1)] * n)[1:])
    attn_here = layout.near(attn_here, 2)
    attn_there = layout.flip(attn_here, 4)
    attn_parts = [attn_here, attn_there, layout.flip(attn_here, 1), layout.flip(attn_there, 1)]
    full_tokens, *attn_parts = after([full_tokens, *attn_parts])
    (ffn_piece,) = after([jnp.concatenate(pieces[2:], axis=1)], full_tokens)
    ffn_all = lax.all_gather(ffn_piece, "mp", axis=0, tiled=False)
    projected = dense(full_tokens, qkv_flat).astype(LOW)
    pairs = w // (2 * HD)
    self_operands = (projected, 0), (projected, pairs), (projected, 2 * pairs)
    home_attended, self_logs = attend(w, *self_operands, True, *SELF_BLOCKS)
    attended_blocks = layout.swap_mp(layout.rows_for(home_attended))
    first_n, first_scale, first_low, *query_blocks = enter_cross(
        tokens, ln_gain, ln_bias, attended_blocks, (self_out, cross_q), attn_parts
    )
    query_blocks = layout.swap_mp(query_blocks)
    memory_there, ffn_all = after([memory, ffn_all], *query_blocks[1:])
    full_memory = lax.all_gather(memory_there, "mp", axis=0, tiled=True)
    ffn_here = jnp.concatenate([lax.dynamic_slice_in_dim(ffn_all, k, 1, 0) for k in order[1:]])
    in_here = layout.near(ffn_here[:, :, :n_hidden], 2)
    out_here = layout.near(ffn_here[:, :, n_hidden:], 4)
    in_there, out_there = layout.flip(in_here, 4), layout.flip(out_here, 2)
    here_others = [layout.flip(in_here, 1), layout.flip(out_here, 1)]
    (cross_queries,) = after([jnp.concatenate(query_blocks)], *here_others)
    cross_pair = dense(full_memory, kv_flat).astype(LOW)
    cross_operands = (cross_queries, 0), (cross_pair, 0), (cross_pair, pairs)
    home_cross, cross_logs = attend(w, *cross_operands, False, *CROSS_BLOCKS)
    in_there, out_there = after([in_there, out_there], home_cross)
    in_parts = [in_here, in_there, here_others[0], layout.flip(in_there, 1)]
    out_parts = [out_here, out_there, here_others[1], layout.flip(out_there, 1)]
    cross_blocks = layout.swap_mp(list(home_cross.reshape(n, rows, w)))
    (
        mixed,
        second_low,
        third_low,
        cross_grad,
        cross_grad_low,
        later_terms,
        activation,
        hidden_grad,
        *cross_grad_blocks,
    ) = feed_forward(
        first_n,
        cotangent,
        ln_gain,
        ln_bias,
        cross_blocks,
        (ffn_in, ffn_out, cross_out),
        in_parts,
        out_parts,
    )
    cross_grad_blocks = layout.swap_mp(cross_grad_blocks)
    cross_attended = jnp.stack(cross_blocks)

    def send(pair, bit):
        return pair[0], layout.flip(pair[1], bit)

    def fold_halves(pair):
        value = layout.fold(*pair)
        middle = value.shape[0] // 2
        return value[:middle], value[middle:]

    lefts = [second_low, third_low, cross_grad_low]
    ffn_grads = functools.partial(
        weight_grads,
        lefts,
        [hidden_grad, activation, cross_attended],
    )
    cuts = (range(0, half), range(half, n))
    ffn_there = [ffn_grads(cut, 1) for cut in cuts]
    ffn_got = [layout.flip(part, 1) for part in ffn_there]
    (cross_attended_grad,) = after([jnp.concatenate(cross_grad_blocks)], *ffn_there)
    cross_queries_grad, cross_keys_grad, cross_values_grad = attend_back(
        w, *cross_operands, cross_attended_grad, home_cross, cross_logs, False, *CROSS_BACK_BLOCKS
    )
    first_terms = layout.swap_mp(list(cross_queries_grad.reshape(n, rows, w)))
    cross_pair_grad = jnp.concatenate([cross_keys_grad, cross_values_grad], axis=-1)
    memory_term = back_dense(cross_pair_grad, kv_flat).astype(LOW)
    memory_grad = lax.psum_scatter(memory_term, "mp", scatter_dimension=0, tiled=True)
    ffn_sums = [ffn_grads(cut, 0, got, bit) for cut, got, bit in zip(cuts, ffn_got, BITS)]
    first_terms[1:] = after(first_terms[1:], memory_term, ffn_sums[0][1], ffn_sums[1][1])
    ffn_sums = [send(pair, bit) for pair, bit in zip(ffn_sums, BITS)]
    self_grad, self_grad_low, first_norm_terms, *attended_grad_blocks = leave_cross(
        cross_grad, ln_gain, first_n, first_scale, first_terms, (self_out, cross_q), attn_parts
    )
    norm_terms = jnp.concatenate([first_norm_terms, later_terms])
    upper = norm_terms.astype(LOW)
    lower = (norm_terms - upper.astype(WIDE)).astype(LOW)
    norm_rows = jnp.concatenate([upper.reshape(-1, w), lower.reshape(-1, w)])
    blocks = layout.swap_mp(
        [jnp.concatenate([block, norm_rows]) for block in attended_grad_blocks]
    )
    attended_grad = layout.in_order([block[:rows] for block in blocks])
    norm_terms = sum(block[rows:].astype(WIDE) for block in blocks)
    norm_terms = norm_terms.reshape(2, -1, model_width).sum(axis=0)
    (attended_grad,) = after([attended_grad], memory_grad)
    queries_grad, keys_grad, values_grad = attend_back(
        w, *self_operands, attended_grad, home_attended, self_logs, True, *SELF_BACK_BLOCKS
    )
    projected_grad = jnp.concatenate([queries_grad, keys_grad, values_grad], axis=-1)
    token_term = back_dense(projected_grad, qkv_flat).astype(LOW)
    (token_term,) = after([token_term], *(got for _, got in ffn_sums))
    token_part = lax.psum_scatter(token_term, "mp", scatter_dimension=0, tiled=True)
    token_grad = (alpha_scale * self_grad + token_part.astype(WIDE)).astype(LOW)
    (self_grad_low,) = after([self_grad_low], token_term)
    attn_grads = functools.partial(
        weight_grads,
        [self_grad_low, first_low],
        [jnp.stack(attended_blocks), jnp.stack(first_terms)],
        range(n),
    )
    ffn_sums = [fold_halves(pair) for pair in ffn_sums]
    ffn_sums = [send(pair, 6 - bit) for pair, bit in zip(ffn_sums, BITS)]
    attn_got = layout.flip(attn_grads(1), 1)
    home_grads = [
        jnp.concatenate(
            [weight_grad(a, cross_pair_grad), weight_grad(b, projected_grad)], axis=1
        ).reshape(CELLS // 2, 1, model_width // CELLS, -1)
        for a, b in zip(layout.core_halves(full_memory), layout.core_halves(full_tokens))
    ]
    home_sum = home_grads[0], layout.flip(home_grads[1], 1)
    attn_sum = send(attn_grads(0, attn_got, 2), 2)
    home_sum = send(fold_halves(home_sum), 4)
    attn_sum = send(fold_halves(attn_sum), 4)
    home_sum = send(fold_halves(home_sum), 2)
    ffn_sums = jnp.concatenate([layout.fold(*pair)[0] for pair in ffn_sums])
    ffn_shard = lax.psum_scatter(ffn_sums, "mp", scatter_dimension=0, tiled=True)
    ffn_shard = layout.to_rows(ffn_shard)[0].astype(WIDE)
    attn_sum = layout.to_rows(layout.fold(*attn_sum)[0])
    attn_sum = [lax.dynamic_index_in_dim(attn_sum, k, 0, keepdims=False) for k in order]
    attn_shard = sum(term.astype(WIDE) for term in layout.swap_mp(attn_sum))
    home_grad = layout.to_rows(layout.fold(*home_sum)[0])[0].astype(WIDE)
    (norm_terms,) = after([norm_terms], ffn_sums)
    sums = layout.sum_dp(norm_terms)
    edges = (n_hidden, 2 * n_hidden)
    ffn_in_grad, ffn_out_grad, cross_out_grad = jnp.split(ffn_shard, edges, axis=1)
    return (
        mixed[:, None],
        token_grad[:, None],
        memory_grad[:, None],
        home_grad[:, 2 * w :].reshape(-1, 3, w),
        attn_shard[:, :w],
        attn_shard[:, w:],
        home_grad[:, : 2 * w].reshape(-1, 2, w),
        cross_out_grad,
        ffn_in_grad,
        ffn_out_grad,
        sums[0::2],
        sums[1::2],
    )


def solution(mesh):
    layout = Layout(mesh.shape["dp"], mesh.shape["mp"])
    in_specs = (
        P("mp", "dp", None),
        P("mp", "dp", None),
        P(None, None, "mp"),
        P(None, "mp"),
        P(None, "mp"),
        P(None, None, "mp"),
        P(None, "mp"),
        P(None, "mp"),
        P(None, "mp"),
        P(),
        P(),
        P("mp", "dp", None),
    )
    out_specs = (
        P("mp", "dp", None),
        P("mp", "dp", None),
        P("mp", "dp", None),
        P("dp", None, "mp"),
        P("dp", "mp"),
        P("dp", "mp"),
        P("dp", None, "mp"),
        P("dp", "mp"),
        P("dp", "mp"),
        P("dp", "mp"),
        P(),
        P(),
    )

    def whole(*arrays):
        return local(layout, *arrays)

    return jax.shard_map(whole, mesh=mesh, in_specs=in_specs, out_specs=out_specs, check_vma=False)
```

```python
import functools
import math

import jax
import jax.numpy as jnp
from jax import lax
from jax.experimental import pallas as pl
from jax.experimental.pallas import tpu as pltpu
from jax.sharding import PartitionSpec as P

HD = 64
CELLS = 8
BITS = (2, 4)
LOW = jnp.bfloat16
WIDE = jnp.float32
SELF_BLOCKS = (512, 512)
CROSS_BLOCKS = (1024, 256)
SELF_BACK_BLOCKS = (512, 512)
CROSS_BACK_BLOCKS = (1024, 256)
VMEM_LIMIT = 56 * 2**20

alpha_scale = 300.0**0.25
norm_eps = 1e-05

NN = (((1,), (0,)), ((), ()))
NT = (((1,), (1,)), ((), ()))
TN = (((0,), (0,)), ((), ()))


def dense(left, weight):
    return jnp.einsum("td,df->tf", left, weight, preferred_element_type=WIDE)


def weight_grad(left, grad):
    return jnp.einsum("td,tf->df", left, grad, preferred_element_type=WIDE).astype(LOW)


def back_dense(grad, weight):
    return jnp.einsum("tf,df->td", grad, weight, preferred_element_type=WIDE)


def mm(left, right, dims):
    return lax.dot_general(left, right, dims, preferred_element_type=WIDE)


def keep_head(value, head):
    at = lax.broadcasted_iota(jnp.int32, value.shape, 1) // HD
    return jnp.where(at == head, value, jnp.zeros_like(value))


def masked(scores, key_begin, query_begin):
    key_at = lax.broadcasted_iota(jnp.int32, scores.shape, 0) + key_begin
    query_at = lax.broadcasted_iota(jnp.int32, scores.shape, 1) + query_begin
    return jnp.where(key_at <= query_at, scores, -1000000000.0)


def key_blocks(body, carry, query_block, key_block, keys, causal):
    if not causal:
        for j in range(keys // key_block):
            carry = body(j, carry, False)
        return carry
    per = query_block // key_block
    begin = pl.program_id(1) * per
    carry = lax.fori_loop(0, begin, lambda j, c: body(j, c, False), carry)
    for e in range(per):
        carry = body(begin + e, carry, True)
    return carry


def take_blocks(refs, rows, query_block, ordered):
    if not ordered:
        return jnp.concatenate([ref[...] for ref in refs], axis=0)
    per = query_block // rows
    parts = []
    for e in range(per):
        place = jnp.bitwise_xor(pl.program_id(1) * per + e, lax.axis_index("mp"))
        part = refs[0][:rows, :].astype(WIDE)
        for k in range(1, len(refs)):
            part = jnp.where(place == k, refs[k][:rows, :].astype(WIDE), part)
        parts.append(part.astype(LOW))
    return jnp.concatenate(parts, axis=0)


def put_blocks(refs, value, ordered):
    rows = refs[0].shape[0]
    if not ordered:
        for k, ref in enumerate(refs):
            ref[...] = value[k * rows : (k + 1) * rows]
        return
    per = value.shape[0] // rows
    for e in range(per):
        place = jnp.bitwise_xor(pl.program_id(1) * per + e, lax.axis_index("mp"))
        for k, ref in enumerate(refs):

            @pl.when(place == k)
            def _(ref=ref, e=e):
                ref[...] = value[e * rows : (e + 1) * rows]


def attend_kernel(*refs, count, key_block, causal):
    q_refs, (k_ref, v_ref, *o_refs, lse_ref) = refs[: -count - 3], refs[-count - 3 :]
    q = q_refs[0][...] if causal else take_blocks(q_refs, 0, 0, False)
    q = q * jnp.asarray(1.0 / math.sqrt(HD), LOW)
    query_block = q.shape[0]
    query_begin = pl.program_id(1) * query_block

    def body(j, carry, diagonal):
        tops, sums, acc = carry[:2], carry[2:4], carry[4]
        at = pl.multiple_of(j * key_block, key_block)
        k, v = k_ref[pl.ds(at, key_block), :], v_ref[pl.ds(at, key_block), :]
        new_tops, new_sums, shrink, parts = [], [], [], []
        for head in (0, 1):
            s = mm(keep_head(k, head), q, NT)
            if diagonal:
                s = masked(s, j * key_block, query_begin)
            top = jnp.maximum(tops[head], jnp.max(s, axis=0, keepdims=True))
            p = jnp.exp(s - top)
            factor = jnp.exp(tops[head] - top)
            new_tops.append(top)
            new_sums.append(sums[head] * factor + jnp.sum(p, axis=0, keepdims=True))
            shrink.append(factor)
            parts.append(mm(keep_head(v, head), p.astype(LOW), TN))
        upper = lax.broadcasted_iota(jnp.int32, acc.shape, 0) < HD
        acc = acc * jnp.where(upper, shrink[0], shrink[1]) + (parts[0] + parts[1])
        return (*new_tops, *new_sums, acc)

    low = jnp.full((1, query_block), -1e30, WIDE)
    zero = jnp.zeros((1, query_block), WIDE)
    start = (low, low, zero, zero, jnp.zeros((2 * HD, query_block), WIDE))
    top0, top1, sum0, sum1, acc = key_blocks(
        body, start, query_block, key_block, k_ref.shape[0], causal
    )
    upper = lax.broadcasted_iota(jnp.int32, acc.shape, 0) < HD
    put_blocks(o_refs, (acc * jnp.where(upper, 1.0 / sum0, 1.0 / sum1)).T.astype(LOW), causal)
    lse_ref[0] = jnp.concatenate(
        [top0 + jnp.log(sum0), top1 + jnp.log(sum1), jnp.zeros((6, query_block), WIDE)], axis=0
    )


def attend_back_kernel(*refs, count, key_block, causal):
    queries = 1 if causal else count
    q_refs, refs = refs[:queries], refs[queries:]
    g_refs, o_refs, refs = refs[:count], refs[count : 2 * count], refs[2 * count :]
    lse_ref, k_ref, v_ref, *dq_refs, dk_ref, dv_ref, dk_acc, dv_acc = refs
    rows, query_block = o_refs[0].shape[0], lse_ref.shape[2]
    query_begin = pl.program_id(1) * query_block

    @pl.when(pl.program_id(1) == 0)
    def _():
        dk_acc[...] = jnp.zeros_like(dk_acc)
        dv_acc[...] = jnp.zeros_like(dv_acc)

    q = q_refs[0][...] if causal else take_blocks(q_refs, 0, 0, False)
    q = q * jnp.asarray(1.0 / math.sqrt(HD), LOW)
    g = take_blocks(g_refs, rows, query_block, causal)
    o = take_blocks(o_refs, rows, query_block, causal)
    q_heads = [keep_head(q, head) for head in (0, 1)]
    g_heads = [keep_head(g, head) for head in (0, 1)]
    picks = lax.broadcasted_iota(jnp.int32, (8, 2 * HD), 1) // HD
    picks = (picks == lax.broadcasted_iota(jnp.int32, (8, 2 * HD), 0)).astype(WIDE)
    inner = lax.dot_general(
        picks,
        g.astype(WIDE) * o.astype(WIDE),
        NT,
        precision=lax.Precision.HIGHEST,
        preferred_element_type=WIDE,
    )
    lse = lse_ref[0]

    def body(j, dq, diagonal):
        at = pl.multiple_of(j * key_block, key_block)
        k, v = k_ref[pl.ds(at, key_block), :], v_ref[pl.ds(at, key_block), :]
        dk, dv = dk_acc[pl.ds(at, key_block), :], dv_acc[pl.ds(at, key_block), :]
        for head in (0, 1):
            k_head = keep_head(k, head)
            s = mm(k_head, q, NT)
            if diagonal:
                s = masked(s, j * key_block, query_begin)
            p = jnp.exp(s - lse[head : head + 1])
            dp = mm(keep_head(v, head), g, NT)
            ds = (p * (dp - inner[head : head + 1])).astype(LOW)
            dv = dv + mm(p.astype(LOW), g_heads[head], NN)
            dk = dk + mm(ds, q_heads[head], NN)
            dq = dq + mm(k_head, ds, TN)
        dk_acc[pl.ds(at, key_block), :] = dk
        dv_acc[pl.ds(at, key_block), :] = dv
        return dq

    dq = key_blocks(
        body, jnp.zeros((2 * HD, query_block), WIDE), query_block, key_block, k_ref.shape[0], causal
    )
    dq = (dq * (1.0 / math.sqrt(HD))).T.astype(LOW)
    if causal:
        dq_refs[0][...] = dq
    else:
        put_blocks(dq_refs, dq, False)

    @pl.when(pl.program_id(1) == pl.num_programs(1) - 1)
    def _():
        dk_ref[...] = dk_acc[...].astype(LOW)
        dv_ref[...] = dv_acc[...].astype(LOW)


def columns_of(rows, first, whole):
    if whole:
        return pl.BlockSpec((rows, 2 * HD), lambda p, i: (0, first + p))
    return pl.BlockSpec((rows, 2 * HD), lambda p, i: (i, first + p))


def attend(width, queries, keys, values, count, causal, query_block, key_block):
    span = keys[0].shape[0]
    if causal:
        seq, operands = queries[0].shape[0], [queries[0]]
        specs = [columns_of(query_block, queries[1], False)]
    else:
        seq, operands = queries[0].shape[0] * count, list(queries)
        specs = [columns_of(seq // count, 0, True)] * count
    rows, pairs = seq // count, width // (2 * HD)
    *blocks, lse = pl.pallas_call(
        functools.partial(attend_kernel, count=count, key_block=key_block, causal=causal),
        grid=(pairs, seq // query_block),
        in_specs=specs + [columns_of(span, keys[1], True), columns_of(span, values[1], True)],
        out_specs=[columns_of(rows, 0, True)] * count
        + [pl.BlockSpec((1, 8, query_block), lambda p, i: (p, 0, i))],
        out_shape=[jax.ShapeDtypeStruct((rows, width), LOW)] * count
        + [jax.ShapeDtypeStruct((pairs, 8, seq), WIDE)],
        compiler_params=pltpu.CompilerParams(vmem_limit_bytes=VMEM_LIMIT),
        cost_estimate=pl.CostEstimate(
            flops=8 * seq * span * width, bytes_accessed=8 * seq * width, transcendentals=0
        ),
        name="attend",
    )(*operands, keys[0], values[0])
    return blocks, lse


def attend_back(width, queries, keys, values, grads, results, lse, causal, query_block, key_block):
    span, seq, count = keys[0].shape[0], lse.shape[2], len(grads)
    rows, pairs = seq // count, width // (2 * HD)
    whole = columns_of(span, 0, True)
    blocks = [columns_of(rows, 0, True)] * count
    if causal:
        operands, specs = [queries[0]], [columns_of(query_block, queries[1], False)]
        out_specs, out_shape = [columns_of(query_block, 0, False)], [(seq, width)]
    else:
        operands, specs = list(queries), blocks
        out_specs, out_shape = blocks, [(rows, width)] * count
    *dq, dk, dv = pl.pallas_call(
        functools.partial(attend_back_kernel, count=count, key_block=key_block, causal=causal),
        grid=(pairs, seq // query_block),
        in_specs=specs
        + [columns_of(grad.shape[0], 0, True) for grad in grads]
        + blocks
        + [
            pl.BlockSpec((1, 8, query_block), lambda p, i: (p, 0, i)),
            columns_of(span, keys[1], True),
            columns_of(span, values[1], True),
        ],
        out_specs=out_specs + [whole, whole],
        out_shape=[
            jax.ShapeDtypeStruct(shape, LOW) for shape in out_shape + [(span, width)] * 2
        ],
        scratch_shapes=[pltpu.VMEM((span, 2 * HD), WIDE), pltpu.VMEM((span, 2 * HD), WIDE)],
        compiler_params=pltpu.CompilerParams(vmem_limit_bytes=VMEM_LIMIT),
        cost_estimate=pl.CostEstimate(
            flops=16 * seq * span * width, bytes_accessed=16 * seq * width, transcendentals=0
        ),
        name="attend_back",
    )(*operands, *grads, *results, lse, keys[0], values[0])
    return (dq[0] if causal else dq), dk, dv


def normalized(value):
    center = value - jnp.mean(value, axis=-1, keepdims=True)
    scale = lax.rsqrt(jnp.mean(center * center, axis=-1, keepdims=True) + norm_eps)
    return center * scale, scale


def norm_back(grad, gain, n, scale):
    e = grad * gain
    mean_e = jnp.mean(e, axis=-1, keepdims=True)
    mean_en = jnp.mean(e * n, axis=-1, keepdims=True)
    terms = jnp.concatenate(
        [jnp.sum(grad * n, axis=0, keepdims=True), jnp.sum(grad, axis=0, keepdims=True)], axis=0
    )
    return (e - mean_e - n * mean_en) * scale, terms


def gelu_with_slope(value):
    c = math.sqrt(2.0 / math.pi)
    square = value * value
    t = jnp.tanh(c * value * (1.0 + 0.044715 * square))
    half = 0.5 * (1.0 + t)
    slope = half + 0.5 * value * (1.0 - t * t) * (c * (1.0 + 3 * 0.044715 * square))
    return value * half, slope


def cell_copies(parts, first, target, sems, pick):
    cell = lax.rem(lax.axis_index("dp"), CELLS)
    rows = target.shape[-2] // CELLS
    copies = []
    for j in range(CELLS):
        part = parts[(j & 1) * 2 + (1 if j & (6 - first) else 0)].at[1 if j & first else 0]
        at = pl.multiple_of(jnp.bitwise_xor(cell, j) * rows, rows)
        copies.append(pltpu.make_async_copy(*pick(part, target, pl.ds(at, rows)), sems.at[j]))
    return copies


def attention_copies(own, parts, weights, sems, begin):
    count, width = weights.shape[0], own[0].shape[1]
    copies = [
        pltpu.make_async_copy(
            ref, weights.at[0, :, i * width : (i + 1) * width], sems.at[CELLS + i]
        )
        for i, ref in enumerate(own)
    ]
    columns = slice(begin, begin + width * len(own))
    return copies + cell_copies(
        parts,
        2,
        weights,
        sems,
        lambda part, to, at: (part.at[:, :, columns], to.at[pl.ds(1, count - 1), at, :]),
    )


def start_all(copies):
    for copy in copies:
        copy.start()


def wait_all(copies):
    for copy in copies:
        copy.wait()


def enter_cross_kernel(
    tokens_ref, gain_ref, bias_ref, *refs, width, count
):
    attended, refs = refs[:count], refs[count:]
    own, parts, refs = refs[:2], refs[2:6], refs[6:]
    n_ref, scale_ref, low_ref = refs[:3]
    queries, (weights, sems) = refs[3 : 3 + count], refs[3 + count :]
    copies = attention_copies(own, parts, weights, sems, 0)
    start_all(copies)
    value = alpha_scale * tokens_ref[...].astype(WIDE)
    wait_all(copies)
    for k in range(count):
        value = value + mm(attended[k][...], weights[k, :, :width], NT)
    n, scale = normalized(value)
    n_ref[...] = n
    scale_ref[...] = jnp.broadcast_to(scale, scale_ref.shape)
    low = (n * gain_ref[0:1, :] + bias_ref[0:1, :]).astype(LOW)
    low_ref[...] = low
    for k in range(count):
        queries[k][...] = mm(low, weights[k, :, width:], NN).astype(LOW)


def term_rows(terms, width):
    rows = [
        terms[t : t + 1, at : at + width]
        for t in range(terms.shape[0])
        for at in range(0, terms.shape[1], width)
    ]
    rows = jnp.concatenate(rows, axis=0)
    upper = rows.astype(LOW)
    return jnp.concatenate([upper, (rows - upper.astype(WIDE)).astype(LOW)], axis=0)


def leave_cross_kernel(
    cross_grad_ref, gain_ref, n_ref, scale_ref, later_ref, *refs, width, count
):
    queries, refs = refs[:count], refs[count:]
    own, parts, refs = refs[:2], refs[2:6], refs[6:]
    self_grad_ref, low_ref = refs[:2]
    grads, (weights, sems) = refs[2 : 2 + count], refs[2 + count :]
    copies = attention_copies(own, parts, weights, sems, 0)
    start_all(copies)
    grad = alpha_scale * cross_grad_ref[...]
    wait_all(copies)
    for k in range(count):
        grad = grad + mm(queries[k][...], weights[k, :, width:], NT)
    self_grad, terms = norm_back(grad, gain_ref[0:1, :], n_ref[...], scale_ref[:, :1])
    terms = term_rows(jnp.concatenate([terms, later_ref[...]], axis=0), width)
    rows = low_ref.shape[0]
    self_grad_ref[...] = self_grad
    low = self_grad.astype(LOW)
    low_ref[...] = low
    for k in range(count):
        grads[k][:rows, :] = mm(low, weights[k, :, :width], NN).astype(LOW)
        grads[k][rows:, :] = terms


def feed_forward_kernel(
    first_n_ref, cotangent_ref, gain_ref, bias_ref, *refs, width, count
):
    attended, refs = refs[:count], refs[count:]
    own, attn_parts, in_parts, out_parts = refs[:3], refs[3:7], refs[7:11], refs[11:15]
    refs = refs[15:]
    mixed_ref, second_low_ref, third_low_ref, cross_grad_ref, cross_low_ref, terms_ref = refs[:6]
    act_ref, hidden_grad_ref = refs[6:8]
    grads, refs = refs[8 : 8 + count], refs[8 + count :]
    w_in, w_out, w_cross, slope_ref, sum_ref, in_sems, out_sems, cross_sems = refs
    hidden = w_in.shape[2]
    chunk = min(512, hidden)

    cross_copies = attention_copies(own[2:], attn_parts, w_cross, cross_sems, 2 * width)
    start_all(cross_copies)
    in_copies = [[pltpu.make_async_copy(own[0], w_in.at[0], in_sems.at[0, 0])]]
    out_copies = [[pltpu.make_async_copy(own[1], w_out.at[0], out_sems.at[0, 0])]]
    for k in range(1, count):
        in_copies.append(
            cell_copies(
                in_parts,
                2,
                w_in,
                in_sems.at[k],
                lambda part, to, at: (part.at[k - 1], to.at[k, at, :]),
            )
        )
        out_copies.append(
            cell_copies(
                out_parts,
                4,
                w_out,
                out_sems.at[k],
                lambda part, to, at: (part.at[k - 1], to.at[k, at, :]),
            )
        )
    for copies in zip(in_copies, out_copies):
        start_all(copies[0])
        start_all(copies[1])

    second = alpha_scale * (first_n_ref[...] * gain_ref[0:1, :] + bias_ref[0:1, :])
    wait_all(cross_copies)
    for k in range(count):
        second = second + mm(attended[k][...], w_cross[k], NT)
    second_n, second_scale = normalized(second)
    second = second_n * gain_ref[1:2, :] + bias_ref[1:2, :]
    second_low = second.astype(LOW)
    second_low_ref[...] = second_low
    sum_ref[...] = alpha_scale * second
    for k in range(count):
        wait_all(in_copies[k])
        for begin in range(0, hidden, chunk):
            cut = slice(begin, begin + chunk)
            value = mm(second_low, w_in[k, :, cut], NN)
            act, slope = gelu_with_slope(value)
            slope_ref[k, :, cut] = slope
            act_ref[k, :, cut] = act.astype(LOW)
        wait_all(out_copies[k])
        sum_ref[...] += mm(act_ref[k], w_out[k], NT)
    third_n, third_scale = normalized(sum_ref[...])
    mixed_ref[...] = (third_n * gain_ref[2:3, :] + bias_ref[2:3, :]).astype(LOW)
    third_grad, third_terms = norm_back(
        cotangent_ref[...].astype(WIDE), gain_ref[2:3, :], third_n, third_scale
    )
    third_low = third_grad.astype(LOW)
    third_low_ref[...] = third_low
    sum_ref[...] = alpha_scale * third_grad
    for k in range(count):
        for begin in range(0, hidden, chunk):
            cut = slice(begin, begin + chunk)
            act_grad = mm(third_low, w_out[k, :, cut], NN).astype(LOW).astype(WIDE)
            hidden_grad_ref[k, :, cut] = (act_grad * slope_ref[k, :, cut]).astype(LOW)
        sum_ref[...] += mm(hidden_grad_ref[k], w_in[k], NT)
    cross_grad, second_terms = norm_back(sum_ref[...], gain_ref[1:2, :], second_n, second_scale)
    terms_ref[...] = jnp.concatenate([second_terms, third_terms], axis=0)
    cross_grad_ref[...] = cross_grad
    cross_low = cross_grad.astype(LOW)
    cross_low_ref[...] = cross_low
    for k in range(count):
        grads[k][...] = mm(cross_low, w_cross[k], NN).astype(LOW)


def call(kernel, operands, streamed, results, scratch, flops, name):
    here, there = pl.BlockSpec(memory_space=pltpu.VMEM), pl.BlockSpec(memory_space=pl.ANY)
    arrays = [*operands, *streamed]
    size = sum(v.size * v.dtype.itemsize for v in arrays)
    return pl.pallas_call(
        kernel,
        in_specs=[here] * len(operands) + [there] * len(streamed),
        out_specs=[here] * len(results),
        out_shape=[jax.ShapeDtypeStruct(shape, dtype) for shape, dtype in results],
        scratch_shapes=scratch,
        compiler_params=pltpu.CompilerParams(vmem_limit_bytes=VMEM_LIMIT),
        cost_estimate=pl.CostEstimate(flops=flops, bytes_accessed=size, transcendentals=0),
        name=name,
    )(*arrays)


def project_kernel(*refs, count):
    blocks, (weight_ref, tokens_ref, out_ref) = refs[:count], refs[count:]
    rows = tokens_ref.shape[0] // count
    for k in range(count):
        at = jnp.bitwise_xor(lax.axis_index("mp"), k) * rows
        at = pl.ds(pl.multiple_of(at, rows), rows)
        block = blocks[k][:rows, :]
        tokens_ref[at, :] = block
        out_ref[at, :] = mm(block, weight_ref[...], NN).astype(LOW)


def project(blocks, rows, weight):
    count, model = len(blocks), blocks[0].shape[1]
    return call(
        functools.partial(project_kernel, count=count),
        [*blocks, weight],
        [],
        [((count * rows, model), LOW), ((count * rows, weight.shape[1]), LOW)],
        [],
        2 * count * rows * model * weight.shape[1],
        "project",
    )


def back_terms_kernel(*refs, count):
    parts, (weight_ref, term_ref, joined_ref) = refs[:count], refs[count:]
    for i, part in enumerate(parts):
        joined_ref[:, i * part.shape[1] : (i + 1) * part.shape[1]] = part[...]
    chunk = term_ref.shape[0] // 4

    @pl.loop(0, 4)
    def _(i):
        at = pl.ds(pl.multiple_of(i * chunk, chunk), chunk)
        term_ref[at, :] = mm(joined_ref[at, :], weight_ref[...], NT).astype(LOW)


def back_terms(parts, weight):
    rows, model = parts[0].shape[0], weight.shape[0]
    return call(
        functools.partial(back_terms_kernel, count=len(parts)),
        [*parts, weight],
        [],
        [((rows, model), LOW), ((rows, weight.shape[1]), LOW)],
        [],
        2 * rows * model * weight.shape[1],
        "back_terms",
    )


def enter_cross(tokens, gain, bias, attended, own, parts):
    rows, model = tokens.shape
    count, width = len(attended), attended[0].shape[1]
    return call(
        functools.partial(enter_cross_kernel, width=width, count=count),
        [tokens, gain, bias, *attended],
        [*own, *parts],
        [((rows, model), WIDE), ((rows, 128), WIDE), ((rows, model), LOW)]
        + [((rows, width), LOW)] * count,
        [
            pltpu.VMEM((count, model, 2 * width), LOW),
            pltpu.SemaphoreType.DMA((CELLS + 2,)),
        ],
        4 * rows * model * width * count,
        "enter_cross",
    )


def leave_cross(cross_grad, gain, n, scale, later_terms, queries, own, parts):
    rows, model = n.shape
    count, width = len(queries), queries[0].shape[1]
    return call(
        functools.partial(leave_cross_kernel, width=width, count=count),
        [cross_grad, gain, n, scale, later_terms, *queries],
        [*own, *parts],
        [((rows, model), WIDE), ((rows, model), LOW)]
        + [((rows + 2 * (2 + later_terms.shape[0]) * model // width, width), LOW)] * count,
        [
            pltpu.VMEM((count, model, 2 * width), LOW),
            pltpu.SemaphoreType.DMA((CELLS + 2,)),
        ],
        4 * rows * model * width * count,
        "leave_cross",
    )


def feed_forward(first_n, cotangent, gain, bias, attended, own, attn_parts, in_parts, out_parts):
    rows, model = first_n.shape
    count, width = len(attended), attended[0].shape[1]
    hidden = own[0].shape[1]
    sems = pltpu.SemaphoreType.DMA((count, CELLS))
    return call(
        functools.partial(feed_forward_kernel, width=width, count=count),
        [first_n, cotangent, gain, bias, *attended],
        [*own, *attn_parts, *in_parts, *out_parts],
        [
            ((rows, model), LOW),
            ((rows, model), LOW),
            ((rows, model), LOW),
            ((rows, model), WIDE),
            ((rows, model), LOW),
            ((4, model), WIDE),
            ((count, rows, hidden), LOW),
            ((count, rows, hidden), LOW),
        ]
        + [((rows, width), LOW)] * count,
        [
            pltpu.VMEM((count, model, hidden), LOW),
            pltpu.VMEM((count, model, hidden), LOW),
            pltpu.VMEM((count, model, width), LOW),
            pltpu.VMEM((count, rows, hidden), WIDE),
            pltpu.VMEM((rows, model), WIDE),
            sems,
            sems,
            pltpu.SemaphoreType.DMA((CELLS + 1,)),
        ],
        8 * rows * model * hidden * count,
        "feed_forward",
    )


def chip_cells(bit):
    keep = [c for c in range(CELLS // 2) if not (2 * c) & bit]
    return keep, [c for c in range(CELLS // 2) if (2 * c) & bit]


def weight_grads_kernel(*refs, count, sizes, begin, other_core, bit):
    lefts, rights, refs = refs[:count], [], refs[count:]
    for size in sizes:
        rights.append(refs[:size])
        refs = refs[size:]
    place = jnp.bitwise_xor(pl.program_id(0) + begin, lax.axis_index("mp"))
    turned = refs[-1]
    block = turned.shape[1] // (CELLS // 2)

    @pl.when(pl.program_id(0) == 0)
    def _():
        cell = lax.rem(lax.axis_index("dp"), CELLS)
        for i, left in enumerate(lefts):
            for c in range(CELLS // 2):
                at = jnp.bitwise_xor(cell, 2 * c + other_core) * block
                columns = left[:, pl.ds(pl.multiple_of(at, block), block)]
                turned[i, c * block : (c + 1) * block, :] = columns.T

    at = 0
    for i, right in enumerate(rights):
        wide = right[0].shape[-1]
        cut = slice(at, at + wide)
        at += wide
        if len(right) == 1:
            operand = right[0][0]
        else:
            operand = right[0][...].astype(WIDE)
            for k in range(1, len(right)):
                operand = jnp.where(place == k, right[k][...].astype(WIDE), operand)
            operand = operand.astype(LOW)
        value = mm(turned[i], operand, NN).reshape(CELLS // 2, block, wide)
        if bit is None:
            refs[0][:, 0, :, cut] = value.astype(LOW)
            continue
        got, *outs = refs[:3]
        for out, cells in zip(outs, chip_cells(bit)):
            for e, c in enumerate(cells):
                out[e, 0, :, cut] = (value[c] + got[c, 0, :, cut].astype(WIDE)).astype(LOW)


def weight_grads(lefts, rights, shards, other_core, got=None, bit=None):
    rows, model = lefts[0].shape
    count, block, cells = len(shards), model // CELLS, CELLS // 2
    rights = [right if isinstance(right, (list, tuple)) else [right] for right in rights]
    width = sum(right[0].shape[-1] for right in rights)

    def right_at(s, mp):
        return jnp.bitwise_xor(s + shards[0], mp[0]), 0, 0

    def whole(cells):
        return pl.BlockSpec((cells, 1, block, width), lambda s, mp: (0, s, 0, 0))

    def result(cells):
        return jax.ShapeDtypeStruct((cells, count, block, width), LOW)

    halves = got is not None
    kernel = functools.partial(
        weight_grads_kernel,
        count=len(lefts),
        sizes=[len(right) for right in rights],
        begin=shards[0],
        other_core=other_core,
        bit=bit,
    )
    right_specs = []
    for right in rights:
        if len(right) == 1:
            right_specs.append(pl.BlockSpec((1, rows, right[0].shape[2]), right_at))
        else:
            right_specs += [pl.BlockSpec(v.shape, lambda s, mp: (0, 0)) for v in right]
    return pl.pallas_call(
        lambda mp, *refs: kernel(*refs),
        grid_spec=pltpu.PrefetchScalarGridSpec(
            num_scalar_prefetch=1,
            grid=(count,),
            in_specs=[pl.BlockSpec((rows, model), lambda s, mp: (0, 0))] * len(lefts)
            + right_specs
            + [whole(cells)] * halves,
            out_specs=[whole(cells // 2)] * 2 if halves else whole(cells),
            scratch_shapes=[pltpu.VMEM((len(lefts), model // 2, rows), LOW)],
        ),
        out_shape=[result(cells // 2)] * 2 if halves else result(cells),
        compiler_params=pltpu.CompilerParams(vmem_limit_bytes=VMEM_LIMIT),
        cost_estimate=pl.CostEstimate(
            flops=rows * model * width * count,
            bytes_accessed=count * model * width,
            transcendentals=0,
        ),
        name="weight_grads",
    )(
        lax.axis_index("mp").astype(jnp.int32).reshape(1),
        *lefts,
        *(v for right in rights for v in right),
        *([got] if halves else []),
    )


def pass_kernel(*refs):
    del refs


def after(values, *others):
    keep = pl.BlockSpec(memory_space=pl.ANY)
    count = len(values)
    return pl.pallas_call(
        pass_kernel,
        in_specs=[keep] * (count + len(others)),
        out_specs=[keep] * count,
        out_shape=[jax.ShapeDtypeStruct(v.shape, v.dtype) for v in values],
        input_output_aliases={i: i for i in range(count)},
        cost_estimate=pl.CostEstimate(flops=0, bytes_accessed=0, transcendentals=0),
        name="order",
    )(*values, *others)


class Layout:
    def __init__(self, dp, mp):
        self.dp, self.mp = dp, mp

    def permute(self, value, move):
        pairs = []
        for d in range(self.dp):
            for m in range(self.mp):
                to_d, to_m = move(d, m)
                pairs.append((d * self.mp + m, to_d * self.mp + to_m))
        return lax.ppermute(value, ("dp", "mp"), pairs)

    def flip(self, value, bits):
        return self.permute(value, lambda d, m: (d ^ bits, m))

    def flip_mp(self, value, bits):
        return self.permute(value, lambda d, m: (d, m ^ bits))

    def cell(self):
        return lax.rem(lax.axis_index("dp"), CELLS)

    def swap_mp(self, blocks):
        return [b if k == 0 else self.flip_mp(b, k) for k, b in enumerate(blocks)]

    def piece(self, slab):
        rows = slab.shape[0] // CELLS
        return lax.dynamic_slice_in_dim(slab, self.cell() * rows, rows, 0)

    def near(self, here, bit):
        return jnp.stack([here, self.flip(here, bit)])

    def core_halves(self, left):
        rows = left.shape[1] // CELLS
        cell = self.cell()
        parts = [
            lax.dynamic_slice_in_dim(left, jnp.bitwise_xor(cell, j) * rows, rows, 1)
            for j in range(CELLS)
        ]
        return jnp.concatenate(parts[0::2], axis=1), jnp.concatenate(parts[1::2], axis=1)

    def fold(self, value, got):
        return (value.astype(WIDE) + got.astype(WIDE)).astype(LOW)

    def to_rows(self, mine):
        groups = self.dp // CELLS
        if groups == 1:
            return mine
        mine = lax.psum_scatter(
            mine,
            "dp",
            scatter_dimension=1,
            tiled=True,
            axis_index_groups=[[g * CELLS + c for g in range(groups)] for c in range(CELLS)],
        )
        return self.permute(mine, lambda d, m: ((d % CELLS) * groups + d // CELLS, m))


def local(
    layout,
    tokens,
    memory,
    self_qkv,
    self_out,
    cross_q,
    cross_kv,
    cross_out,
    ffn_in,
    ffn_out,
    ln_gain,
    ln_bias,
    cotangent,
):
    model_width = tokens.shape[2]
    w = self_out.shape[1]
    n = layout.mp
    tokens, memory, cotangent = (
        v.reshape(v.shape[0], model_width) for v in (tokens, memory, cotangent)
    )
    rows = tokens.shape[0]
    qkv_flat = self_qkv.reshape(model_width, 3 * w)
    kv_flat = cross_kv.reshape(model_width, 2 * w)
    n_hidden = ffn_in.shape[1]
    half = n // 2
    order = [jnp.bitwise_xor(lax.axis_index("mp"), k) for k in range(n)]

    full_tokens = lax.all_gather(tokens, "mp", axis=0, tiled=True)
    pieces = [layout.piece(v) for v in (self_out, cross_q, cross_out, ffn_in, ffn_out)]
    attn_here = jnp.stack(layout.swap_mp([jnp.concatenate(pieces[:3], axis=1)] * n)[1:])
    attn_here = layout.near(attn_here, 2)
    attn_there = layout.flip(attn_here, 4)
    (full_tokens,) = after([full_tokens], attn_here, qkv_flat, kv_flat)
    (ffn_piece,) = after([jnp.concatenate(pieces[3:], axis=1)], full_tokens)
    ffn_all = lax.all_gather(ffn_piece, "mp", axis=0, tiled=False)
    projected = dense(full_tokens, qkv_flat).astype(LOW)
    pairs = w // (2 * HD)
    self_operands = (projected, 0), (projected, pairs), (projected, 2 * pairs)
    home_attended, self_logs = attend(w, *self_operands, n, True, *SELF_BLOCKS)
    *home_attended, attn_there = after([*home_attended, attn_there])
    attn_parts = [attn_here, attn_there, layout.flip(attn_here, 1), layout.flip(attn_there, 1)]
    attended_blocks = layout.swap_mp(home_attended)
    first_n, first_scale, first_low, *query_blocks = enter_cross(
        tokens, ln_gain, ln_bias, attended_blocks, (self_out, cross_q), attn_parts
    )
    memory_there, ffn_all = after([memory, ffn_all], *query_blocks)
    full_memory = lax.all_gather(memory_there, "mp", axis=0, tiled=True)
    ffn_here = jnp.concatenate([lax.dynamic_slice_in_dim(ffn_all, k, 1, 0) for k in order[1:]])
    in_here = layout.near(ffn_here[:, :, :n_hidden], 2)
    out_here = layout.near(ffn_here[:, :, n_hidden:], 4)
    in_there, out_there = layout.flip(in_here, 4), layout.flip(out_here, 2)
    here_others = [layout.flip(in_here, 1), layout.flip(out_here, 1)]
    query_blocks = layout.swap_mp(after(query_blocks, *here_others))
    cross_pair = dense(full_memory, kv_flat).astype(LOW)
    cross_operands = query_blocks, (cross_pair, 0), (cross_pair, pairs)
    home_cross, cross_logs = attend(w, *cross_operands, n, False, *CROSS_BLOCKS)
    in_there, out_there = after([in_there, out_there], home_cross[0])
    in_parts = [in_here, in_there, here_others[0], layout.flip(in_there, 1)]
    out_parts = [out_here, out_there, here_others[1], layout.flip(out_there, 1)]
    cross_blocks = layout.swap_mp(home_cross)
    (
        mixed,
        second_low,
        third_low,
        cross_grad,
        cross_grad_low,
        later_terms,
        activation,
        hidden_grad,
        *cross_grad_blocks,
    ) = feed_forward(
        first_n,
        cotangent,
        ln_gain,
        ln_bias,
        cross_blocks,
        (ffn_in, ffn_out, cross_out),
        attn_parts,
        in_parts,
        out_parts,
    )
    cross_grad_blocks = layout.swap_mp(cross_grad_blocks)

    def send(pair, bit):
        return pair[0], layout.flip(pair[1], bit)

    def fold_halves(pair):
        value = layout.fold(*pair)
        middle = value.shape[0] // 2
        return value[:middle], value[middle:]

    lefts = [second_low, third_low, cross_grad_low]
    ffn_grads = functools.partial(
        weight_grads,
        lefts,
        [hidden_grad, activation, cross_blocks],
    )
    cuts = (range(0, half), range(half, n))
    ffn_there = [ffn_grads(cut, 1) for cut in cuts]
    ffn_got = [layout.flip(part, 1) for part in ffn_there]
    cross_grad_blocks[1:] = after(cross_grad_blocks[1:], *ffn_there)
    cross_queries_grad, cross_keys_grad, cross_values_grad = attend_back(
        w, *cross_operands, cross_grad_blocks, home_cross, cross_logs, False, *CROSS_BACK_BLOCKS
    )
    first_terms = layout.swap_mp(cross_queries_grad)
    memory_term, cross_pair_grad = back_terms([cross_keys_grad, cross_values_grad], kv_flat)
    memory_grad = lax.psum_scatter(memory_term, "mp", scatter_dimension=0, tiled=True)
    ffn_got = after(ffn_got, *first_terms[2:])
    ffn_sums = [ffn_grads(cut, 0, got, bit) for cut, got, bit in zip(cuts, ffn_got, BITS)]
    first_terms[1:] = after(first_terms[1:], memory_term, ffn_sums[0][1], ffn_sums[1][1])
    ffn_sums = [send(pair, bit) for pair, bit in zip(ffn_sums, BITS)]
    self_grad, self_grad_low, *attended_grad_blocks = leave_cross(
        cross_grad,
        ln_gain,
        first_n,
        first_scale,
        later_terms,
        first_terms,
        (self_out, cross_q),
        attn_parts,
    )
    blocks = layout.swap_mp(attended_grad_blocks)
    norm_terms = sum(block[rows:].astype(WIDE) for block in blocks)
    norm_terms = norm_terms.reshape(2, -1, model_width).sum(axis=0)

    def send_with_terms(there, terms, bit):
        upper = terms.astype(LOW)
        both = jnp.concatenate([upper, (terms - upper.astype(WIDE)).astype(LOW)])
        width = there.shape[-1]
        both = jnp.pad(both, ((0, 16 - both.shape[0]), (0, width - both.shape[1])))
        got = layout.flip(jnp.concatenate([there.reshape(-1, width), both]), bit)
        count = terms.shape[0]
        more = got[-16:, : terms.shape[1]].astype(WIDE)
        terms = terms + more[:count] + more[count : 2 * count]
        return got[:-16].reshape(there.shape), terms

    blocks[1:] = after(blocks[1:], memory_grad)
    queries_grad, keys_grad, values_grad = attend_back(
        w, *self_operands, blocks, home_attended, self_logs, True, *SELF_BACK_BLOCKS
    )
    token_term, projected_grad = back_terms([queries_grad, keys_grad, values_grad], qkv_flat)
    chip_got = [got for _, got in ffn_sums]
    token_part = lax.psum_scatter(token_term, "mp", scatter_dimension=0, tiled=True)
    token_grad = (alpha_scale * self_grad + token_part.astype(WIDE)).astype(LOW)
    (self_grad_low,) = after([self_grad_low], token_term, *chip_got)
    attn_grads = functools.partial(
        weight_grads,
        [self_grad_low, first_low],
        [attended_blocks, first_terms],
        range(n),
    )
    ffn_sums = [fold_halves(pair) for pair in ffn_sums]
    ffn_sums = [send(pair, 6 - bit) for pair, bit in zip(ffn_sums, BITS)]
    attn_got = layout.flip(attn_grads(1), 1)
    attn_sum = attn_grads(0, attn_got, 2)
    cross_pair_grad, projected_grad, full_memory = after(
        [cross_pair_grad, projected_grad, full_memory], attn_sum[1]
    )
    home_grads = [
        jnp.concatenate(
            [weight_grad(a, cross_pair_grad), weight_grad(b, projected_grad)], axis=1
        ).reshape(CELLS // 2, 1, model_width // CELLS, -1)
        for a, b in zip(layout.core_halves(full_memory), layout.core_halves(full_tokens))
    ]
    home_got, norm_terms = send_with_terms(home_grads[1], norm_terms, 1)
    ffn_got = after([got for _, got in ffn_sums], attn_sum[1], *home_grads)
    ffn_sums = [(here, got) for (here, _), got in zip(ffn_sums, ffn_got)]
    attn_sum = send(attn_sum, 2)
    home_here, home_there = fold_halves((home_grads[0], home_got))
    home_got, norm_terms = send_with_terms(home_there, norm_terms, 4)
    home_here, home_there = fold_halves((home_here, home_got))
    home_got, sums = send_with_terms(home_there, norm_terms, 2)
    attn_here, attn_there = fold_halves(attn_sum)
    (attn_there,) = after([attn_there], home_got)
    attn_sum = send((attn_here, attn_there), 4)
    home_sum = home_here, home_got
    ffn_sums = jnp.concatenate([layout.fold(*pair)[0] for pair in ffn_sums])
    ffn_shard = lax.psum_scatter(ffn_sums, "mp", scatter_dimension=0, tiled=True)
    home_grad = layout.to_rows(layout.fold(*home_sum)[0])[0].astype(WIDE)
    kv_grad = home_grad[:, : 2 * w].reshape(-1, 2, w)
    qkv_grad = home_grad[:, 2 * w :].reshape(-1, 3, w)
    attn_sum = layout.to_rows(layout.fold(*attn_sum)[0])
    attn_sum = [lax.dynamic_index_in_dim(attn_sum, k, 0, keepdims=False) for k in order]
    attn_sum = layout.swap_mp(attn_sum)
    attn_shard = sum(term.astype(WIDE) for term in attn_sum)
    (ffn_shard,) = after([ffn_shard], attn_shard, token_grad, kv_grad, qkv_grad, sums)
    ffn_shard = layout.to_rows(ffn_shard)[0].astype(WIDE)
    edges = (n_hidden, 2 * n_hidden)
    ffn_in_grad, ffn_out_grad, cross_out_grad = jnp.split(ffn_shard, edges, axis=1)
    return (
        mixed[:, None],
        token_grad[:, None],
        memory_grad[:, None],
        qkv_grad,
        attn_shard[:, :w],
        attn_shard[:, w:],
        kv_grad,
        cross_out_grad,
        ffn_in_grad,
        ffn_out_grad,
        sums[0::2],
        sums[1::2],
    )


def solution(mesh):
    layout = Layout(mesh.shape["dp"], mesh.shape["mp"])
    in_specs = (
        P("mp", "dp", None),
        P("mp", "dp", None),
        P(None, None, "mp"),
        P(None, "mp"),
        P(None, "mp"),
        P(None, None, "mp"),
        P(None, "mp"),
        P(None, "mp"),
        P(None, "mp"),
        P(),
        P(),
        P("mp", "dp", None),
    )
    out_specs = (
        P("mp", "dp", None),
        P("mp", "dp", None),
        P("mp", "dp", None),
        P("dp", None, "mp"),
        P("dp", "mp"),
        P("dp", "mp"),
        P("dp", None, "mp"),
        P("dp", "mp"),
        P("dp", "mp"),
        P("dp", "mp"),
        P(),
        P(),
    )

    def whole(*arrays):
        return local(layout, *arrays)

    return jax.shard_map(whole, mesh=mesh, in_specs=in_specs, out_specs=out_specs, check_vma=False)
```

```python
import functools
import math

import jax
import jax.numpy as jnp
from jax import lax
from jax.experimental import pallas as pl
from jax.experimental.pallas import tpu as pltpu
from jax.sharding import PartitionSpec as P

HD = 64
CELLS = 8
BITS = (2, 4)
LOW = jnp.bfloat16
WIDE = jnp.float32
SELF_BLOCKS = (512, 512)
CROSS_BLOCKS = (1024, 256)
SELF_BACK_BLOCKS = (512, 512)
CROSS_BACK_BLOCKS = (1024, 256)
VMEM_LIMIT = 56 * 2**20

alpha_scale = 300.0**0.25
norm_eps = 1e-05

NN = (((1,), (0,)), ((), ()))
NT = (((1,), (1,)), ((), ()))
TN = (((0,), (0,)), ((), ()))


def dense(left, weight):
    return jnp.einsum("td,df->tf", left, weight, preferred_element_type=WIDE)


def weight_grad(left, grad):
    return jnp.einsum("td,tf->df", left, grad, preferred_element_type=WIDE).astype(LOW)


def back_dense(grad, weight):
    return jnp.einsum("tf,df->td", grad, weight, preferred_element_type=WIDE)


def mm(left, right, dims):
    return lax.dot_general(left, right, dims, preferred_element_type=WIDE)


def keep_head(value, head):
    at = lax.broadcasted_iota(jnp.int32, value.shape, 1) // HD
    return jnp.where(at == head, value, jnp.zeros_like(value))


def masked(scores, key_begin, query_begin):
    key_at = lax.broadcasted_iota(jnp.int32, scores.shape, 0) + key_begin
    query_at = lax.broadcasted_iota(jnp.int32, scores.shape, 1) + query_begin
    return jnp.where(key_at <= query_at, scores, -1000000000.0)


def key_blocks(body, carry, query_block, key_block, keys, causal):
    if not causal:
        for j in range(keys // key_block):
            carry = body(j, carry, False)
        return carry
    per = query_block // key_block
    begin = pl.program_id(1) * per
    carry = lax.fori_loop(0, begin, lambda j, c: body(j, c, False), carry)
    for e in range(per):
        carry = body(begin + e, carry, True)
    return carry


def take_blocks(refs, rows, query_block, ordered):
    if not ordered:
        return jnp.concatenate([ref[...] for ref in refs], axis=0)
    per = query_block // rows
    parts = []
    for e in range(per):
        place = jnp.bitwise_xor(pl.program_id(1) * per + e, lax.axis_index("mp"))
        part = refs[0][:rows, :].astype(WIDE)
        for k in range(1, len(refs)):
            part = jnp.where(place == k, refs[k][:rows, :].astype(WIDE), part)
        parts.append(part.astype(LOW))
    return jnp.concatenate(parts, axis=0)


def put_blocks(refs, value, ordered):
    rows = refs[0].shape[0]
    if not ordered:
        for k, ref in enumerate(refs):
            ref[...] = value[k * rows : (k + 1) * rows]
        return
    per = value.shape[0] // rows
    for e in range(per):
        place = jnp.bitwise_xor(pl.program_id(1) * per + e, lax.axis_index("mp"))
        for k, ref in enumerate(refs):

            @pl.when(place == k)
            def _(ref=ref, e=e):
                ref[...] = value[e * rows : (e + 1) * rows]


def attend_kernel(*refs, count, key_block, causal):
    q_refs, (k_ref, v_ref, *o_refs, lse_ref) = refs[: -count - 3], refs[-count - 3 :]
    q = q_refs[0][...] if causal else take_blocks(q_refs, 0, 0, False)
    q = q * jnp.asarray(1.0 / math.sqrt(HD), LOW)
    query_block = q.shape[0]
    query_begin = pl.program_id(1) * query_block

    def body(j, carry, diagonal):
        tops, sums, acc = carry[:2], carry[2:4], carry[4]
        at = pl.multiple_of(j * key_block, key_block)
        k, v = k_ref[pl.ds(at, key_block), :], v_ref[pl.ds(at, key_block), :]
        new_tops, new_sums, shrink, parts = [], [], [], []
        for head in (0, 1):
            s = mm(keep_head(k, head), q, NT)
            if diagonal:
                s = masked(s, j * key_block, query_begin)
            top = jnp.maximum(tops[head], jnp.max(s, axis=0, keepdims=True))
            p = jnp.exp(s - top)
            factor = jnp.exp(tops[head] - top)
            new_tops.append(top)
            new_sums.append(sums[head] * factor + jnp.sum(p, axis=0, keepdims=True))
            shrink.append(factor)
            parts.append(mm(keep_head(v, head), p.astype(LOW), TN))
        upper = lax.broadcasted_iota(jnp.int32, acc.shape, 0) < HD
        acc = acc * jnp.where(upper, shrink[0], shrink[1]) + (parts[0] + parts[1])
        return (*new_tops, *new_sums, acc)

    low = jnp.full((1, query_block), -1e30, WIDE)
    zero = jnp.zeros((1, query_block), WIDE)
    start = (low, low, zero, zero, jnp.zeros((2 * HD, query_block), WIDE))
    top0, top1, sum0, sum1, acc = key_blocks(
        body, start, query_block, key_block, k_ref.shape[0], causal
    )
    upper = lax.broadcasted_iota(jnp.int32, acc.shape, 0) < HD
    put_blocks(o_refs, (acc * jnp.where(upper, 1.0 / sum0, 1.0 / sum1)).T.astype(LOW), causal)
    lse_ref[0] = jnp.concatenate(
        [top0 + jnp.log(sum0), top1 + jnp.log(sum1), jnp.zeros((6, query_block), WIDE)], axis=0
    )


def attend_back_kernel(*refs, count, key_block, causal):
    queries = 1 if causal else count
    q_refs, refs = refs[:queries], refs[queries:]
    g_refs, o_refs, refs = refs[:count], refs[count : 2 * count], refs[2 * count :]
    lse_ref, k_ref, v_ref, *dq_refs, dk_ref, dv_ref, dk_acc, dv_acc = refs
    rows, query_block = o_refs[0].shape[0], lse_ref.shape[2]
    query_begin = pl.program_id(1) * query_block

    @pl.when(pl.program_id(1) == 0)
    def _():
        dk_acc[...] = jnp.zeros_like(dk_acc)
        dv_acc[...] = jnp.zeros_like(dv_acc)

    q = q_refs[0][...] if causal else take_blocks(q_refs, 0, 0, False)
    q = q * jnp.asarray(1.0 / math.sqrt(HD), LOW)
    g = take_blocks(g_refs, rows, query_block, causal)
    o = take_blocks(o_refs, rows, query_block, causal)
    q_heads = [keep_head(q, head) for head in (0, 1)]
    g_heads = [keep_head(g, head) for head in (0, 1)]
    picks = lax.broadcasted_iota(jnp.int32, (8, 2 * HD), 1) // HD
    picks = (picks == lax.broadcasted_iota(jnp.int32, (8, 2 * HD), 0)).astype(WIDE)
    inner = lax.dot_general(
        picks,
        g.astype(WIDE) * o.astype(WIDE),
        NT,
        precision=lax.Precision.HIGHEST,
        preferred_element_type=WIDE,
    )
    lse = lse_ref[0]

    def body(j, dq, diagonal):
        at = pl.multiple_of(j * key_block, key_block)
        k, v = k_ref[pl.ds(at, key_block), :], v_ref[pl.ds(at, key_block), :]
        dk, dv = dk_acc[pl.ds(at, key_block), :], dv_acc[pl.ds(at, key_block), :]
        for head in (0, 1):
            k_head = keep_head(k, head)
            s = mm(k_head, q, NT)
            if diagonal:
                s = masked(s, j * key_block, query_begin)
            p = jnp.exp(s - lse[head : head + 1])
            dp = mm(keep_head(v, head), g, NT)
            ds = (p * (dp - inner[head : head + 1])).astype(LOW)
            dv = dv + mm(p.astype(LOW), g_heads[head], NN)
            dk = dk + mm(ds, q_heads[head], NN)
            dq = dq + mm(k_head, ds, TN)
        dk_acc[pl.ds(at, key_block), :] = dk
        dv_acc[pl.ds(at, key_block), :] = dv
        return dq

    dq = key_blocks(
        body, jnp.zeros((2 * HD, query_block), WIDE), query_block, key_block, k_ref.shape[0], causal
    )
    dq = (dq * (1.0 / math.sqrt(HD))).T.astype(LOW)
    if causal:
        dq_refs[0][...] = dq
    else:
        put_blocks(dq_refs, dq, False)

    @pl.when(pl.program_id(1) == pl.num_programs(1) - 1)
    def _():
        dk_ref[...] = dk_acc[...].astype(LOW)
        dv_ref[...] = dv_acc[...].astype(LOW)


def columns_of(rows, first, whole):
    if whole:
        return pl.BlockSpec((rows, 2 * HD), lambda p, i: (0, first + p))
    return pl.BlockSpec((rows, 2 * HD), lambda p, i: (i, first + p))


def attend(width, queries, keys, values, count, causal, query_block, key_block):
    span = keys[0].shape[0]
    if causal:
        seq, operands = queries[0].shape[0], [queries[0]]
        specs = [columns_of(query_block, queries[1], False)]
    else:
        seq, operands = queries[0].shape[0] * count, list(queries)
        specs = [columns_of(seq // count, 0, True)] * count
    rows, pairs = seq // count, width // (2 * HD)
    *blocks, lse = pl.pallas_call(
        functools.partial(attend_kernel, count=count, key_block=key_block, causal=causal),
        grid=(pairs, seq // query_block),
        in_specs=specs + [columns_of(span, keys[1], True), columns_of(span, values[1], True)],
        out_specs=[columns_of(rows, 0, True)] * count
        + [pl.BlockSpec((1, 8, query_block), lambda p, i: (p, 0, i))],
        out_shape=[jax.ShapeDtypeStruct((rows, width), LOW)] * count
        + [jax.ShapeDtypeStruct((pairs, 8, seq), WIDE)],
        compiler_params=pltpu.CompilerParams(vmem_limit_bytes=VMEM_LIMIT),
        cost_estimate=pl.CostEstimate(
            flops=8 * seq * span * width, bytes_accessed=8 * seq * width, transcendentals=0
        ),
        name="attend",
    )(*operands, keys[0], values[0])
    return blocks, lse


def attend_back(width, queries, keys, values, grads, results, lse, causal, query_block, key_block):
    span, seq, count = keys[0].shape[0], lse.shape[2], len(grads)
    rows, pairs = seq // count, width // (2 * HD)
    whole = columns_of(span, 0, True)
    blocks = [columns_of(rows, 0, True)] * count
    if causal:
        operands, specs = [queries[0]], [columns_of(query_block, queries[1], False)]
        out_specs, out_shape = [columns_of(query_block, 0, False)], [(seq, width)]
    else:
        operands, specs = list(queries), blocks
        out_specs, out_shape = blocks, [(rows, width)] * count
    *dq, dk, dv = pl.pallas_call(
        functools.partial(attend_back_kernel, count=count, key_block=key_block, causal=causal),
        grid=(pairs, seq // query_block),
        in_specs=specs
        + [columns_of(grad.shape[0], 0, True) for grad in grads]
        + blocks
        + [
            pl.BlockSpec((1, 8, query_block), lambda p, i: (p, 0, i)),
            columns_of(span, keys[1], True),
            columns_of(span, values[1], True),
        ],
        out_specs=out_specs + [whole, whole],
        out_shape=[
            jax.ShapeDtypeStruct(shape, LOW) for shape in out_shape + [(span, width)] * 2
        ],
        scratch_shapes=[pltpu.VMEM((span, 2 * HD), WIDE), pltpu.VMEM((span, 2 * HD), WIDE)],
        compiler_params=pltpu.CompilerParams(vmem_limit_bytes=VMEM_LIMIT),
        cost_estimate=pl.CostEstimate(
            flops=16 * seq * span * width, bytes_accessed=16 * seq * width, transcendentals=0
        ),
        name="attend_back",
    )(*operands, *grads, *results, lse, keys[0], values[0])
    return (dq[0] if causal else dq), dk, dv


def normalized(value):
    center = value - jnp.mean(value, axis=-1, keepdims=True)
    scale = lax.rsqrt(jnp.mean(center * center, axis=-1, keepdims=True) + norm_eps)
    return center * scale, scale


def norm_back(grad, gain, n, scale):
    e = grad * gain
    mean_e = jnp.mean(e, axis=-1, keepdims=True)
    mean_en = jnp.mean(e * n, axis=-1, keepdims=True)
    terms = jnp.concatenate(
        [jnp.sum(grad * n, axis=0, keepdims=True), jnp.sum(grad, axis=0, keepdims=True)], axis=0
    )
    return (e - mean_e - n * mean_en) * scale, terms


def gelu_with_slope(value):
    c = math.sqrt(2.0 / math.pi)
    square = value * value
    t = jnp.tanh(c * value * (1.0 + 0.044715 * square))
    half = 0.5 * (1.0 + t)
    slope = half + 0.5 * value * (1.0 - t * t) * (c * (1.0 + 3 * 0.044715 * square))
    return value * half, slope


def cell_copies(parts, first, target, sems, pick):
    cell = lax.rem(lax.axis_index("dp"), CELLS)
    rows = target.shape[-2] // CELLS
    copies = []
    for j in range(CELLS):
        part = parts[(j & 1) * 2 + (1 if j & (6 - first) else 0)].at[1 if j & first else 0]
        at = pl.multiple_of(jnp.bitwise_xor(cell, j) * rows, rows)
        copies.append(pltpu.make_async_copy(*pick(part, target, pl.ds(at, rows)), sems.at[j]))
    return copies


def attention_copies(own, parts, weights, sems, begin):
    count, width = weights.shape[0], own[0].shape[1]
    copies = [
        pltpu.make_async_copy(
            ref, weights.at[0, :, i * width : (i + 1) * width], sems.at[CELLS + i]
        )
        for i, ref in enumerate(own)
    ]
    columns = slice(begin, begin + width * len(own))
    return copies + cell_copies(
        parts,
        2,
        weights,
        sems,
        lambda part, to, at: (part.at[:, :, columns], to.at[pl.ds(1, count - 1), at, :]),
    )


def start_all(copies):
    for copy in copies:
        copy.start()


def wait_all(copies):
    for copy in copies:
        copy.wait()


def enter_cross_kernel(
    tokens_ref, gain_ref, bias_ref, *refs, width, count
):
    attended, refs = refs[:count], refs[count:]
    own, parts, refs = refs[:2], refs[2:6], refs[6:]
    n_ref, scale_ref, low_ref = refs[:3]
    queries, (weights, sems) = refs[3 : 3 + count], refs[3 + count :]
    copies = attention_copies(own, parts, weights, sems, 0)
    start_all(copies)
    value = alpha_scale * tokens_ref[...].astype(WIDE)
    wait_all(copies)
    for k in range(count):
        value = value + mm(attended[k][...], weights[k, :, :width], NT)
    n, scale = normalized(value)
    n_ref[...] = n
    scale_ref[...] = jnp.broadcast_to(scale, scale_ref.shape)
    low = (n * gain_ref[0:1, :] + bias_ref[0:1, :]).astype(LOW)
    low_ref[...] = low
    for k in range(count):
        queries[k][...] = mm(low, weights[k, :, width:], NN).astype(LOW)


def term_rows(terms, width):
    rows = [
        terms[t : t + 1, at : at + width]
        for t in range(terms.shape[0])
        for at in range(0, terms.shape[1], width)
    ]
    rows = jnp.concatenate(rows, axis=0)
    upper = rows.astype(LOW)
    return jnp.concatenate([upper, (rows - upper.astype(WIDE)).astype(LOW)], axis=0)


def leave_cross_kernel(
    cross_grad_ref, gain_ref, n_ref, scale_ref, later_ref, *refs, width, count
):
    queries, refs = refs[:count], refs[count:]
    own, parts, refs = refs[:2], refs[2:6], refs[6:]
    self_grad_ref, low_ref = refs[:2]
    grads, (weights, sems) = refs[2 : 2 + count], refs[2 + count :]
    copies = attention_copies(own, parts, weights, sems, 0)
    start_all(copies)
    grad = alpha_scale * cross_grad_ref[...]
    wait_all(copies)
    for k in range(count):
        grad = grad + mm(queries[k][...], weights[k, :, width:], NT)
    self_grad, terms = norm_back(grad, gain_ref[0:1, :], n_ref[...], scale_ref[:, :1])
    terms = term_rows(jnp.concatenate([terms, later_ref[...]], axis=0), width)
    rows = low_ref.shape[0]
    self_grad_ref[...] = self_grad
    low = self_grad.astype(LOW)
    low_ref[...] = low
    for k in range(count):
        grads[k][:rows, :] = mm(low, weights[k, :, :width], NN).astype(LOW)
        grads[k][rows:, :] = terms


def feed_forward_kernel(
    first_n_ref, cotangent_ref, gain_ref, bias_ref, *refs, width, count
):
    attended, refs = refs[:count], refs[count:]
    own, attn_parts, in_parts, out_parts = refs[:3], refs[3:7], refs[7:11], refs[11:15]
    refs = refs[15:]
    mixed_ref, second_low_ref, third_low_ref, cross_grad_ref, cross_low_ref, terms_ref = refs[:6]
    act_ref, hidden_grad_ref = refs[6:8]
    grads, refs = refs[8 : 8 + count], refs[8 + count :]
    w_in, w_out, w_cross, slope_ref, sum_ref, in_sems, out_sems, cross_sems = refs
    hidden = w_in.shape[2]
    chunk = min(512, hidden)

    cross_copies = attention_copies(own[2:], attn_parts, w_cross, cross_sems, 2 * width)
    start_all(cross_copies)
    in_copies = [[pltpu.make_async_copy(own[0], w_in.at[0], in_sems.at[0, 0])]]
    out_copies = [[pltpu.make_async_copy(own[1], w_out.at[0], out_sems.at[0, 0])]]
    for k in range(1, count):
        in_copies.append(
            cell_copies(
                in_parts,
                2,
                w_in,
                in_sems.at[k],
                lambda part, to, at: (part.at[k - 1], to.at[k, at, :]),
            )
        )
        out_copies.append(
            cell_copies(
                out_parts,
                4,
                w_out,
                out_sems.at[k],
                lambda part, to, at: (part.at[k - 1], to.at[k, at, :]),
            )
        )
    for copies in zip(in_copies, out_copies):
        start_all(copies[0])
        start_all(copies[1])

    second = alpha_scale * (first_n_ref[...] * gain_ref[0:1, :] + bias_ref[0:1, :])
    wait_all(cross_copies)
    for k in range(count):
        second = second + mm(attended[k][...], w_cross[k], NT)
    second_n, second_scale = normalized(second)
    second = second_n * gain_ref[1:2, :] + bias_ref[1:2, :]
    second_low = second.astype(LOW)
    second_low_ref[...] = second_low
    sum_ref[...] = alpha_scale * second
    for k in range(count):
        wait_all(in_copies[k])
        for begin in range(0, hidden, chunk):
            cut = slice(begin, begin + chunk)
            value = mm(second_low, w_in[k, :, cut], NN)
            act, slope = gelu_with_slope(value)
            slope_ref[k, :, cut] = slope
            act_ref[k, :, cut] = act.astype(LOW)
        wait_all(out_copies[k])
        sum_ref[...] += mm(act_ref[k], w_out[k], NT)
    third_n, third_scale = normalized(sum_ref[...])
    mixed_ref[...] = (third_n * gain_ref[2:3, :] + bias_ref[2:3, :]).astype(LOW)
    third_grad, third_terms = norm_back(
        cotangent_ref[...].astype(WIDE), gain_ref[2:3, :], third_n, third_scale
    )
    third_low = third_grad.astype(LOW)
    third_low_ref[...] = third_low
    sum_ref[...] = alpha_scale * third_grad
    for k in range(count):
        for begin in range(0, hidden, chunk):
            cut = slice(begin, begin + chunk)
            act_grad = mm(third_low, w_out[k, :, cut], NN).astype(LOW).astype(WIDE)
            hidden_grad_ref[k, :, cut] = (act_grad * slope_ref[k, :, cut]).astype(LOW)
        sum_ref[...] += mm(hidden_grad_ref[k], w_in[k], NT)
    cross_grad, second_terms = norm_back(sum_ref[...], gain_ref[1:2, :], second_n, second_scale)
    terms_ref[...] = jnp.concatenate([second_terms, third_terms], axis=0)
    cross_grad_ref[...] = cross_grad
    cross_low = cross_grad.astype(LOW)
    cross_low_ref[...] = cross_low
    for k in range(count):
        grads[k][...] = mm(cross_low, w_cross[k], NN).astype(LOW)


def call(kernel, operands, streamed, results, scratch, flops, name):
    here, there = pl.BlockSpec(memory_space=pltpu.VMEM), pl.BlockSpec(memory_space=pl.ANY)
    arrays = [*operands, *streamed]
    size = sum(v.size * v.dtype.itemsize for v in arrays)
    return pl.pallas_call(
        kernel,
        in_specs=[here] * len(operands) + [there] * len(streamed),
        out_specs=[here] * len(results),
        out_shape=[jax.ShapeDtypeStruct(shape, dtype) for shape, dtype in results],
        scratch_shapes=scratch,
        compiler_params=pltpu.CompilerParams(vmem_limit_bytes=VMEM_LIMIT),
        cost_estimate=pl.CostEstimate(flops=flops, bytes_accessed=size, transcendentals=0),
        name=name,
    )(*arrays)


def project_kernel(*refs, count):
    blocks, (weight_ref, tokens_ref, out_ref) = refs[:count], refs[count:]
    rows = tokens_ref.shape[0] // count
    for k in range(count):
        at = jnp.bitwise_xor(lax.axis_index("mp"), k) * rows
        at = pl.ds(pl.multiple_of(at, rows), rows)
        block = blocks[k][:rows, :]
        tokens_ref[at, :] = block
        out_ref[at, :] = mm(block, weight_ref[...], NN).astype(LOW)


def project(blocks, rows, weight):
    count, model = len(blocks), blocks[0].shape[1]
    return call(
        functools.partial(project_kernel, count=count),
        [*blocks, weight],
        [],
        [((count * rows, model), LOW), ((count * rows, weight.shape[1]), LOW)],
        [],
        2 * count * rows * model * weight.shape[1],
        "project",
    )


def back_terms_kernel(*refs, count):
    parts, (weight_ref, term_ref, joined_ref) = refs[:count], refs[count:]
    for i, part in enumerate(parts):
        joined_ref[:, i * part.shape[1] : (i + 1) * part.shape[1]] = part[...]
    chunk = term_ref.shape[0] // 4

    @pl.loop(0, 4)
    def _(i):
        at = pl.ds(pl.multiple_of(i * chunk, chunk), chunk)
        term_ref[at, :] = mm(joined_ref[at, :], weight_ref[...], NT).astype(LOW)


def back_terms(parts, weight):
    rows, model = parts[0].shape[0], weight.shape[0]
    return call(
        functools.partial(back_terms_kernel, count=len(parts)),
        [*parts, weight],
        [],
        [((rows, model), LOW), ((rows, weight.shape[1]), LOW)],
        [],
        2 * rows * model * weight.shape[1],
        "back_terms",
    )


def enter_cross(tokens, gain, bias, attended, own, parts):
    rows, model = tokens.shape
    count, width = len(attended), attended[0].shape[1]
    return call(
        functools.partial(enter_cross_kernel, width=width, count=count),
        [tokens, gain, bias, *attended],
        [*own, *parts],
        [((rows, model), WIDE), ((rows, 128), WIDE), ((rows, model), LOW)]
        + [((rows, width), LOW)] * count,
        [
            pltpu.VMEM((count, model, 2 * width), LOW),
            pltpu.SemaphoreType.DMA((CELLS + 2,)),
        ],
        4 * rows * model * width * count,
        "enter_cross",
    )


def leave_cross(cross_grad, gain, n, scale, later_terms, queries, own, parts):
    rows, model = n.shape
    count, width = len(queries), queries[0].shape[1]
    return call(
        functools.partial(leave_cross_kernel, width=width, count=count),
        [cross_grad, gain, n, scale, later_terms, *queries],
        [*own, *parts],
        [((rows, model), WIDE), ((rows, model), LOW)]
        + [((rows + 2 * (2 + later_terms.shape[0]) * model // width, width), LOW)] * count,
        [
            pltpu.VMEM((count, model, 2 * width), LOW),
            pltpu.SemaphoreType.DMA((CELLS + 2,)),
        ],
        4 * rows * model * width * count,
        "leave_cross",
    )


def feed_forward(first_n, cotangent, gain, bias, attended, own, attn_parts, in_parts, out_parts):
    rows, model = first_n.shape
    count, width = len(attended), attended[0].shape[1]
    hidden = own[0].shape[1]
    sems = pltpu.SemaphoreType.DMA((count, CELLS))
    return call(
        functools.partial(feed_forward_kernel, width=width, count=count),
        [first_n, cotangent, gain, bias, *attended],
        [*own, *attn_parts, *in_parts, *out_parts],
        [
            ((rows, model), LOW),
            ((rows, model), LOW),
            ((rows, model), LOW),
            ((rows, model), WIDE),
            ((rows, model), LOW),
            ((4, model), WIDE),
            ((count, rows, hidden), LOW),
            ((count, rows, hidden), LOW),
        ]
        + [((rows, width), LOW)] * count,
        [
            pltpu.VMEM((count, model, hidden), LOW),
            pltpu.VMEM((count, model, hidden), LOW),
            pltpu.VMEM((count, model, width), LOW),
            pltpu.VMEM((count, rows, hidden), WIDE),
            pltpu.VMEM((rows, model), WIDE),
            sems,
            sems,
            pltpu.SemaphoreType.DMA((CELLS + 1,)),
        ],
        8 * rows * model * hidden * count,
        "feed_forward",
    )


def chip_cells(bit):
    keep = [c for c in range(CELLS // 2) if not (2 * c) & bit]
    return keep, [c for c in range(CELLS // 2) if (2 * c) & bit]


def weight_grads_kernel(*refs, count, sizes, begin, other_core, bit):
    lefts, rights, refs = refs[:count], [], refs[count:]
    for size in sizes:
        rights.append(refs[:size])
        refs = refs[size:]
    place = jnp.bitwise_xor(pl.program_id(0) + begin, lax.axis_index("mp"))
    turned = refs[-1]
    block = turned.shape[1] // (CELLS // 2)

    @pl.when(pl.program_id(0) == 0)
    def _():
        cell = lax.rem(lax.axis_index("dp"), CELLS)
        for i, left in enumerate(lefts):
            for c in range(CELLS // 2):
                at = jnp.bitwise_xor(cell, 2 * c + other_core) * block
                columns = left[:, pl.ds(pl.multiple_of(at, block), block)]
                turned[i, c * block : (c + 1) * block, :] = columns.T

    at = 0
    for i, right in enumerate(rights):
        wide = right[0].shape[-1]
        cut = slice(at, at + wide)
        at += wide
        if len(right) == 1:
            operand = right[0][0]
        else:
            operand = right[0][...].astype(WIDE)
            for k in range(1, len(right)):
                operand = jnp.where(place == k, right[k][...].astype(WIDE), operand)
            operand = operand.astype(LOW)
        value = mm(turned[i], operand, NN).reshape(CELLS // 2, block, wide)
        if bit is None:
            refs[0][:, 0, :, cut] = value.astype(LOW)
            continue
        got, *outs = refs[:3]
        for out, cells in zip(outs, chip_cells(bit)):
            for e, c in enumerate(cells):
                out[e, 0, :, cut] = (value[c] + got[c, 0, :, cut].astype(WIDE)).astype(LOW)


def weight_grads(lefts, rights, shards, other_core, got=None, bit=None):
    rows, model = lefts[0].shape
    count, block, cells = len(shards), model // CELLS, CELLS // 2
    rights = [right if isinstance(right, (list, tuple)) else [right] for right in rights]
    width = sum(right[0].shape[-1] for right in rights)

    def right_at(s, mp):
        return jnp.bitwise_xor(s + shards[0], mp[0]), 0, 0

    def whole(cells):
        return pl.BlockSpec((cells, 1, block, width), lambda s, mp: (0, s, 0, 0))

    def result(cells):
        return jax.ShapeDtypeStruct((cells, count, block, width), LOW)

    halves = got is not None
    kernel = functools.partial(
        weight_grads_kernel,
        count=len(lefts),
        sizes=[len(right) for right in rights],
        begin=shards[0],
        other_core=other_core,
        bit=bit,
    )
    right_specs = []
    for right in rights:
        if len(right) == 1:
            right_specs.append(pl.BlockSpec((1, rows, right[0].shape[2]), right_at))
        else:
            right_specs += [pl.BlockSpec(v.shape, lambda s, mp: (0, 0)) for v in right]
    return pl.pallas_call(
        lambda mp, *refs: kernel(*refs),
        grid_spec=pltpu.PrefetchScalarGridSpec(
            num_scalar_prefetch=1,
            grid=(count,),
            in_specs=[pl.BlockSpec((rows, model), lambda s, mp: (0, 0))] * len(lefts)
            + right_specs
            + [whole(cells)] * halves,
            out_specs=[whole(cells // 2)] * 2 if halves else whole(cells),
            scratch_shapes=[pltpu.VMEM((len(lefts), model // 2, rows), LOW)],
        ),
        out_shape=[result(cells // 2)] * 2 if halves else result(cells),
        compiler_params=pltpu.CompilerParams(vmem_limit_bytes=VMEM_LIMIT),
        cost_estimate=pl.CostEstimate(
            flops=rows * model * width * count,
            bytes_accessed=count * model * width,
            transcendentals=0,
        ),
        name="weight_grads",
    )(
        lax.axis_index("mp").astype(jnp.int32).reshape(1),
        *lefts,
        *(v for right in rights for v in right),
        *([got] if halves else []),
    )


def pass_kernel(*refs):
    del refs


def after(values, *others):
    keep = pl.BlockSpec(memory_space=pl.ANY)
    count = len(values)
    return pl.pallas_call(
        pass_kernel,
        in_specs=[keep] * (count + len(others)),
        out_specs=[keep] * count,
        out_shape=[jax.ShapeDtypeStruct(v.shape, v.dtype) for v in values],
        input_output_aliases={i: i for i in range(count)},
        cost_estimate=pl.CostEstimate(flops=0, bytes_accessed=0, transcendentals=0),
        name="order",
    )(*values, *others)


class Layout:
    def __init__(self, dp, mp):
        self.dp, self.mp = dp, mp

    def permute(self, value, move):
        pairs = []
        for d in range(self.dp):
            for m in range(self.mp):
                to_d, to_m = move(d, m)
                pairs.append((d * self.mp + m, to_d * self.mp + to_m))
        return lax.ppermute(value, ("dp", "mp"), pairs)

    def flip(self, value, bits):
        return self.permute(value, lambda d, m: (d ^ bits, m))

    def flip_mp(self, value, bits):
        return self.permute(value, lambda d, m: (d, m ^ bits))

    def cell(self):
        return lax.rem(lax.axis_index("dp"), CELLS)

    def swap_mp(self, blocks):
        return [b if k == 0 else self.flip_mp(b, k) for k, b in enumerate(blocks)]

    def piece(self, slab):
        rows = slab.shape[0] // CELLS
        return lax.dynamic_slice_in_dim(slab, self.cell() * rows, rows, 0)

    def near(self, here, bit):
        return jnp.stack([here, self.flip(here, bit)])

    def core_halves(self, left):
        rows = left.shape[1] // CELLS
        cell = self.cell()
        parts = [
            lax.dynamic_slice_in_dim(left, jnp.bitwise_xor(cell, j) * rows, rows, 1)
            for j in range(CELLS)
        ]
        return jnp.concatenate(parts[0::2], axis=1), jnp.concatenate(parts[1::2], axis=1)

    def fold(self, value, got):
        return (value.astype(WIDE) + got.astype(WIDE)).astype(LOW)

    def to_rows(self, mine):
        groups = self.dp // CELLS
        if groups == 1:
            return mine
        mine = lax.psum_scatter(
            mine,
            "dp",
            scatter_dimension=1,
            tiled=True,
            axis_index_groups=[[g * CELLS + c for g in range(groups)] for c in range(CELLS)],
        )
        return self.permute(mine, lambda d, m: ((d % CELLS) * groups + d // CELLS, m))


def local(
    layout,
    tokens,
    memory,
    self_qkv,
    self_out,
    cross_q,
    cross_kv,
    cross_out,
    ffn_in,
    ffn_out,
    ln_gain,
    ln_bias,
    cotangent,
):
    model_width = tokens.shape[2]
    w = self_out.shape[1]
    n = layout.mp
    tokens, memory, cotangent = (
        v.reshape(v.shape[0], model_width) for v in (tokens, memory, cotangent)
    )
    rows = tokens.shape[0]
    qkv_flat = self_qkv.reshape(model_width, 3 * w)
    kv_flat = cross_kv.reshape(model_width, 2 * w)
    n_hidden = ffn_in.shape[1]
    half = n // 2
    order = [jnp.bitwise_xor(lax.axis_index("mp"), k) for k in range(n)]

    full_tokens = lax.all_gather(tokens, "mp", axis=0, tiled=True)
    pieces = [layout.piece(v) for v in (self_out, cross_q, cross_out, ffn_in, ffn_out)]
    attn_here = jnp.stack(layout.swap_mp([jnp.concatenate(pieces[:3], axis=1)] * n)[1:])
    attn_here = layout.near(attn_here, 2)
    attn_there = layout.flip(attn_here, 4)
    (full_tokens,) = after([full_tokens], attn_here, qkv_flat, kv_flat)
    (ffn_piece,) = after([jnp.concatenate(pieces[3:], axis=1)], full_tokens)
    ffn_all = lax.all_gather(ffn_piece, "mp", axis=0, tiled=False)
    projected = dense(full_tokens, qkv_flat).astype(LOW)
    pairs = w // (2 * HD)
    self_operands = (projected, 0), (projected, pairs), (projected, 2 * pairs)
    home_attended, self_logs = attend(w, *self_operands, n, True, *SELF_BLOCKS)
    *home_attended, attn_there = after([*home_attended, attn_there])
    attn_parts = [attn_here, attn_there, layout.flip(attn_here, 1), layout.flip(attn_there, 1)]
    attended_blocks = layout.swap_mp(home_attended)
    first_n, first_scale, first_low, *query_blocks = enter_cross(
        tokens, ln_gain, ln_bias, attended_blocks, (self_out, cross_q), attn_parts
    )
    memory_there, ffn_all = after([memory, ffn_all], *query_blocks)
    full_memory = lax.all_gather(memory_there, "mp", axis=0, tiled=True)
    ffn_here = jnp.concatenate([lax.dynamic_slice_in_dim(ffn_all, k, 1, 0) for k in order[1:]])
    in_here = layout.near(ffn_here[:, :, :n_hidden], 2)
    out_here = layout.near(ffn_here[:, :, n_hidden:], 4)
    in_there, out_there = layout.flip(in_here, 4), layout.flip(out_here, 2)
    here_others = [layout.flip(in_here, 1), layout.flip(out_here, 1)]
    query_blocks = layout.swap_mp(after(query_blocks, *here_others))
    cross_pair = dense(full_memory, kv_flat).astype(LOW)
    cross_operands = query_blocks, (cross_pair, 0), (cross_pair, pairs)
    home_cross, cross_logs = attend(w, *cross_operands, n, False, *CROSS_BLOCKS)
    in_there, out_there = after([in_there, out_there], home_cross[0])
    in_parts = [in_here, in_there, here_others[0], layout.flip(in_there, 1)]
    out_parts = [out_here, out_there, here_others[1], layout.flip(out_there, 1)]
    cross_blocks = layout.swap_mp(home_cross)
    (
        mixed,
        second_low,
        third_low,
        cross_grad,
        cross_grad_low,
        later_terms,
        activation,
        hidden_grad,
        *cross_grad_blocks,
    ) = feed_forward(
        first_n,
        cotangent,
        ln_gain,
        ln_bias,
        cross_blocks,
        (ffn_in, ffn_out, cross_out),
        attn_parts,
        in_parts,
        out_parts,
    )
    cross_grad_blocks = layout.swap_mp(cross_grad_blocks)

    def send(pair, bit):
        return pair[0], layout.flip(pair[1], bit)

    def fold_halves(pair):
        value = layout.fold(*pair)
        middle = value.shape[0] // 2
        return value[:middle], value[middle:]

    lefts = [second_low, third_low, cross_grad_low]
    ffn_grads = functools.partial(
        weight_grads,
        lefts,
        [hidden_grad, activation, cross_blocks],
    )
    cuts = (range(0, half), range(half, n))
    ffn_there = [ffn_grads(cut, 1) for cut in cuts]
    ffn_got = [layout.flip(part, 1) for part in ffn_there]
    cross_grad_blocks[1:] = after(cross_grad_blocks[1:], *ffn_there)
    cross_queries_grad, cross_keys_grad, cross_values_grad = attend_back(
        w, *cross_operands, cross_grad_blocks, home_cross, cross_logs, False, *CROSS_BACK_BLOCKS
    )
    first_terms = layout.swap_mp(cross_queries_grad)
    memory_term, cross_pair_grad = back_terms([cross_keys_grad, cross_values_grad], kv_flat)
    memory_grad = lax.psum_scatter(memory_term, "mp", scatter_dimension=0, tiled=True)
    ffn_got = after(ffn_got, *first_terms[2:])
    ffn_sums = [ffn_grads(cut, 0, got, bit) for cut, got, bit in zip(cuts, ffn_got, BITS)]
    first_terms[1:] = after(first_terms[1:], memory_term, ffn_sums[0][1], ffn_sums[1][1])
    ffn_sums = [send(pair, bit) for pair, bit in zip(ffn_sums, BITS)]
    self_grad, self_grad_low, *attended_grad_blocks = leave_cross(
        cross_grad,
        ln_gain,
        first_n,
        first_scale,
        later_terms,
        first_terms,
        (self_out, cross_q),
        attn_parts,
    )
    blocks = layout.swap_mp(attended_grad_blocks)
    norm_terms = sum(block[rows:].astype(WIDE) for block in blocks)
    norm_terms = norm_terms.reshape(2, -1, model_width).sum(axis=0)

    def send_with_terms(there, terms, bit):
        upper = terms.astype(LOW)
        both = jnp.concatenate([upper, (terms - upper.astype(WIDE)).astype(LOW)])
        width = there.shape[-1]
        both = jnp.pad(both, ((0, 16 - both.shape[0]), (0, width - both.shape[1])))
        got = layout.flip(jnp.concatenate([there.reshape(-1, width), both]), bit)
        count = terms.shape[0]
        more = got[-16:, : terms.shape[1]].astype(WIDE)
        terms = terms + more[:count] + more[count : 2 * count]
        return got[:-16].reshape(there.shape), terms

    blocks[1:] = after(blocks[1:], memory_grad)
    queries_grad, keys_grad, values_grad = attend_back(
        w, *self_operands, blocks, home_attended, self_logs, True, *SELF_BACK_BLOCKS
    )
    token_term, projected_grad = back_terms([queries_grad, keys_grad, values_grad], qkv_flat)
    chip_got = [got for _, got in ffn_sums]
    token_part = lax.psum_scatter(token_term, "mp", scatter_dimension=0, tiled=True)
    token_grad = (alpha_scale * self_grad + token_part.astype(WIDE)).astype(LOW)
    (self_grad_low,) = after([self_grad_low], token_term, *chip_got)
    attn_grads = functools.partial(
        weight_grads,
        [self_grad_low, first_low],
        [attended_blocks, first_terms],
        range(n),
    )
    ffn_sums = [fold_halves(pair) for pair in ffn_sums]
    ffn_sums = [send(pair, 6 - bit) for pair, bit in zip(ffn_sums, BITS)]
    attn_got = layout.flip(attn_grads(1), 1)
    attn_sum = attn_grads(0, attn_got, 2)
    cross_pair_grad, projected_grad, full_memory = after(
        [cross_pair_grad, projected_grad, full_memory], attn_sum[1]
    )
    home_grads = [
        jnp.concatenate(
            [weight_grad(a, cross_pair_grad), weight_grad(b, projected_grad)], axis=1
        ).reshape(CELLS // 2, 1, model_width // CELLS, -1)
        for a, b in zip(layout.core_halves(full_memory), layout.core_halves(full_tokens))
    ]
    home_got, norm_terms = send_with_terms(home_grads[1], norm_terms, 1)
    ffn_got = after([got for _, got in ffn_sums], attn_sum[1], *home_grads)
    ffn_sums = [(here, got) for (here, _), got in zip(ffn_sums, ffn_got)]
    attn_sum = send(attn_sum, 2)
    home_here, home_there = fold_halves((home_grads[0], home_got))
    home_got, norm_terms = send_with_terms(home_there, norm_terms, 4)
    attn_sum = attn_sum[0], *after([attn_sum[1]], home_got)
    home_here, home_there = fold_halves((home_here, home_got))
    home_got, sums = send_with_terms(home_there, norm_terms, 2)
    attn_here, attn_there = fold_halves(attn_sum)
    attn_sum = send((attn_here, attn_there), 4)
    home_sum = home_here, home_got
    ffn_sums = jnp.concatenate([layout.fold(*pair)[0] for pair in ffn_sums])
    ffn_shard = lax.psum_scatter(ffn_sums, "mp", scatter_dimension=0, tiled=True)
    home_grad = layout.to_rows(layout.fold(*home_sum)[0])[0].astype(WIDE)
    kv_grad = home_grad[:, : 2 * w].reshape(-1, 2, w)
    qkv_grad = home_grad[:, 2 * w :].reshape(-1, 3, w)
    attn_sum = layout.to_rows(layout.fold(*attn_sum)[0])
    attn_sum = [lax.dynamic_index_in_dim(attn_sum, k, 0, keepdims=False) for k in order]
    attn_sum = layout.swap_mp(attn_sum)
    attn_shard = sum(term.astype(WIDE) for term in attn_sum)
    (ffn_shard,) = after([ffn_shard], attn_shard, token_grad, kv_grad, qkv_grad, sums)
    ffn_shard = layout.to_rows(ffn_shard)[0].astype(WIDE)
    edges = (n_hidden, 2 * n_hidden)
    ffn_in_grad, ffn_out_grad, cross_out_grad = jnp.split(ffn_shard, edges, axis=1)
    return (
        mixed[:, None],
        token_grad[:, None],
        memory_grad[:, None],
        qkv_grad,
        attn_shard[:, :w],
        attn_shard[:, w:],
        kv_grad,
        cross_out_grad,
        ffn_in_grad,
        ffn_out_grad,
        sums[0::2],
        sums[1::2],
    )


def solution(mesh):
    layout = Layout(mesh.shape["dp"], mesh.shape["mp"])
    in_specs = (
        P("mp", "dp", None),
        P("mp", "dp", None),
        P(None, None, "mp"),
        P(None, "mp"),
        P(None, "mp"),
        P(None, None, "mp"),
        P(None, "mp"),
        P(None, "mp"),
        P(None, "mp"),
        P(),
        P(),
        P("mp", "dp", None),
    )
    out_specs = (
        P("mp", "dp", None),
        P("mp", "dp", None),
        P("mp", "dp", None),
        P("dp", None, "mp"),
        P("dp", "mp"),
        P("dp", "mp"),
        P("dp", None, "mp"),
        P("dp", "mp"),
        P("dp", "mp"),
        P("dp", "mp"),
        P(),
        P(),
    )

    def whole(*arrays):
        return local(layout, *arrays)

    return jax.shard_map(whole, mesh=mesh, in_specs=in_specs, out_specs=out_specs, check_vma=False)
```
